256 devices in a mesh: dp: 8 (over z), expert: 32 (over y, x, core).
Axes of the slice: x: 4, y: 4, z: 8, core: 2. Of those that a mesh axis runs over, the one named last changes fastest.
Arguments:
- tokens: bfloat16 [32768, 3584], P(('dp', 'expert')), may hold values from -6 to 6
- cotangent: bfloat16 [32768, 3584], P(('dp', 'expert')), may hold values from -6 to 6
- routes: int32 [32768, 1], P(('dp', 'expert')), may hold values from 0 to 7; in each aligned block of 128 rows (0 to 127, 128 to 255, ...) at most 20 rows name the same one
- gates: float32 [32768, 1], P(('dp', 'expert')), may hold values from 0.1 to 1
- w_gate_up: bfloat16 [2, 3584, 8192], P(None, 'dp', 'expert'), may hold values from -0.09375 to 0.09375
- w_down: bfloat16 [8192, 3584], P('expert', 'dp'), may hold values from -0.1875 to 0.1875
- m_gate_up: float32 [2, 3584, 8192], P(None, 'dp', 'expert'), may hold values from -2 to 2
- v_gate_up: float32 [2, 3584, 8192], P(None, 'dp', 'expert'), may hold values from 0.01 to 1
- m_down: float32 [8192, 3584], P('expert', 'dp'), may hold values from -2 to 2
- v_down: float32 [8192, 3584], P('expert', 'dp'), may hold values from 0.01 to 1
Outputs:
- outputs: bfloat16 [32768, 3584], P(('dp', 'expert'))
- input_grads: bfloat16 [32768, 3584], P(('dp', 'expert'))
- new_w_gate_up: bfloat16 [2, 3584, 8192], P(None, 'dp', 'expert')
- new_m_gate_up: float32 [2, 3584, 8192], P(None, 'dp', 'expert')
- new_v_gate_up: float32 [2, 3584, 8192], P(None, 'dp', 'expert')
- new_w_down: bfloat16 [8192, 3584], P('expert', 'dp')
- new_m_down: float32 [8192, 3584], P('expert', 'dp')
- new_v_down: float32 [8192, 3584], P('expert', 'dp')
The draws below stay inside these ranges and needn't reach their ends.
Inputs may be any that keep to these rules, and one draw needn't show every extreme that they name: `routes`: among the rows of one device, no expert is named more than 20 times, and one expert is named exactly 20 times in some devices' rows.
All inputs are finite; a program needn't handle non-finite values.
Results may differ from the reference program's by a relative error of at most 0.014.
Values may be sent and summed in bfloat16 or wider, within the bound.
No kernel may reach another device: no remote copies, remote signals or barrier semaphores. Data moves between devices by JAX's collectives and lax.ppermute only.
A program may use at most 128 MiB of HBM per device.

```python
import math
import jax
import jax.numpy as jnp
import numpy as np
from jax import lax

D = 3584
FF = 1024
EXPERTS = 8
ROUTED = 1
TOK_DEV = 128
CAPACITY = 20
TOKENS = 32768
N_DP = 8
N_EXPERT = 32


def level_of(own_key, extent, pieces, least, largest):
    level = 1.0
    for position, shards_of in pieces:
        steps = jax.random.uniform(jax.random.fold_in(jax.random.fold_in(own_key, 6), position), (shards_of,), jnp.float32, least / len(pieces), largest / len(pieces))
        level = level * jnp.repeat(jnp.exp(steps), extent[position] // shards_of).reshape((-1,) + (1,) * (len(extent) - 1 - position))
    return level


def deal_out(key, own, number, rows, amount, top, bound, slope):
    order = jax.random.permutation(key, amount)
    crowded, ordinary = portions_of(amount, rows * top, bound, slope, True), portions_of(amount, rows * top, bound, slope, False)
    places = jnp.arange(amount)

    def named(lengths, rotation):
        used = int((lengths > 0).sum())
        fixed = max(1, used // 4)
        passed = fixed + (places - fixed + rotation * (used - fixed)) % max(1, amount - fixed)
        return jnp.zeros((amount,), jnp.int32).at[order[jnp.where(places < fixed, places, passed)]].set(jnp.asarray(lengths, jnp.int32))

    lengths = jnp.where(number % 4 == 0, named(crowded, number // 4), named(ordinary, number - number // 4 - 1))
    mixed = jax.random.permutation(jax.random.fold_in(own, 3), amount)
    giver, taker = mixed[0:amount // 2 * 2:2], mixed[1:amount // 2 * 2:2]
    slack = jnp.minimum(lengths[giver] - 1, bound - lengths[taker]) // 2
    slack = jnp.where((giver == order[0]) | (taker == order[0]) | (lengths[taker] == 0), 0, jnp.maximum(slack, 0))
    passed = jax.random.randint(jax.random.fold_in(own, 4), (amount // 2,), 0, 1 << 20) % (slack + 1)
    lengths = lengths.at[giver].add(-passed).at[taker].add(passed)
    items = jnp.searchsorted(jnp.cumsum(lengths), jnp.arange(rows * top), side="right").astype(jnp.int32)
    listing = items.reshape(top, rows).T
    listing = listing[jax.random.permutation(jax.random.fold_in(own, 1), rows)]
    rotation = jax.random.randint(jax.random.fold_in(own, 2), (rows, 1), 0, top)
    return jnp.take_along_axis(listing, (jnp.arange(top)[None, :] + rotation) % top, axis=1)


def portions_of(count, total, limit, slope, full):
    portions = [(1 << 20) // math.isqrt(rank ** slope) + 1 for rank in range(1, count + 1)]
    largest = limit if full else min(limit, max(-(-total // count), total * portions[0] // sum(portions)))
    least = 1 if total - largest >= count - 1 else 0
    counts, spare = [largest] + [least] * (count - 1), total - largest - least * (count - 1)
    while spare > 0:
        movable = [i for i in range(1, count) if counts[i] < largest] or [i for i in range(1, count) if counts[i] < limit]
        pool, budget = sum([portions[i] for i in movable]), spare
        for i in movable:
            addition = min(limit - counts[i], max(1, budget * portions[i] // pool), spare)
            counts[i] = counts[i] + addition
            spare = spare - addition
    return np.array(counts)


def centred(key, dims, deviation, reach, cuts=(), kind=jnp.bfloat16):
    factor_of = level_of(key, dims, cuts, -0.22, 0.18) if cuts else 1.0
    array = jax.random.normal(key, dims, jnp.float32) * deviation * factor_of
    return jnp.minimum(jnp.maximum(array, -reach), reach).astype(kind)


def setup_inputs(seed: int = 0) -> dict:
    keys = jax.random.split(jax.random.key(seed), 11)
    tokens = centred(keys[0], (TOKENS, D), 1.0, 6.0, ((0, 256),))
    cotangent = centred(keys[1], (TOKENS, D), 1.0, 6.0, ((0, 256),))
    routes_keys = jax.random.split(jax.random.fold_in(keys[2], 1), TOKENS // TOK_DEV)
    routes_turns = jax.random.permutation(jax.random.fold_in(keys[2], 3), TOKENS // TOK_DEV)
    routes = jax.vmap(lambda own, number: deal_out(jax.random.fold_in(keys[2], 2), own, number, TOK_DEV, EXPERTS, ROUTED, CAPACITY, 1))(routes_keys, routes_turns).reshape((TOKENS, ROUTED))
    gates = jnp.clip(0.1 + 0.9 * jax.random.uniform(keys[3], (TOKENS, ROUTED), jnp.float32) ** level_of(keys[3], (TOKENS, ROUTED), ((0, 256),), -0.2, 0.2), 0.1, 1.0)
    w_gate_up = centred(keys[4], (2, D, EXPERTS * FF), D ** -0.5, 0.09375, ((1, 8), (2, 32)))
    w_down = centred(keys[5], (EXPERTS * FF, D), FF ** -0.5, 0.1875, ((0, 32), (1, 8)))
    m_gate_up = centred(keys[6], (2, D, EXPERTS * FF), 0.3, 2.0, ((1, 8), (2, 32)), jnp.float32)
    v_gate_up = jnp.clip(jnp.exp(math.log(1.0) - 4.6051702 * jax.random.uniform(keys[7], (2, D, EXPERTS * FF), jnp.float32) ** level_of(keys[7], (2, D, EXPERTS * FF), ((1, 8), (2, 32)), -0.2, 0.2)), 0.01, 1.0)
    m_down = centred(keys[8], (EXPERTS * FF, D), 0.3, 2.0, ((0, 32), (1, 8)), jnp.float32)
    v_down = jnp.clip(jnp.exp(math.log(1.0) - 4.6051702 * jax.random.uniform(keys[9], (EXPERTS * FF, D), jnp.float32) ** level_of(keys[9], (EXPERTS * FF, D), ((0, 32), (1, 8)), -0.2, 0.2)), 0.01, 1.0)
    return dict(tokens=tokens, cotangent=cotangent, routes=routes, gates=gates, w_gate_up=w_gate_up, w_down=w_down, m_gate_up=m_gate_up, v_gate_up=v_gate_up, m_down=m_down, v_down=v_down)


first_decay = 0.9
second_decay = 0.95
first_correction = 1.0 - 0.9 ** 50 * 0.9 ** 50
second_correction = 1.0 - 0.95 ** 50 * 0.95 ** 50
learn_rate = 0.01
adam_epsilon = 1e-08

def round_trip(value):
    return lax.optimization_barrier(value.astype(jnp.bfloat16)).astype(jnp.float32)

def slot_positions(flat_routes):
    experts_iota = jnp.arange(EXPERTS, dtype=jnp.int32)
    onehot = (flat_routes[:, None] == experts_iota[None, :]).astype(jnp.int32)
    before = jnp.cumsum(onehot, axis=0) - onehot
    slots = lax.optimization_barrier(jnp.sum(before * onehot, axis=1))
    return (flat_routes * CAPACITY + slots).astype(jnp.int32)

def adam_update(weight, moment, second, grad_sum):
    grad = grad_sum * (TOKENS * ROUTED / EXPERTS) ** (-0.5)
    moment_new = first_decay * moment + (1.0 - first_decay) * grad
    second_new = second_decay * second + (1.0 - second_decay) * grad * grad
    update = moment_new / first_correction / (jnp.sqrt(second_new / second_correction) + adam_epsilon)
    weight_new = (weight.astype(jnp.float32) - learn_rate * update).astype(jnp.bfloat16)
    return (weight_new, moment_new, second_new)

def reference(tokens, cotangent, routes, gates, w_gate_up, w_down, m_gate_up, v_gate_up, m_down, v_down):
    group = N_EXPERT // EXPERTS
    block_width = FF // group
    per_device = TOK_DEV * ROUTED
    tok = tokens.reshape(N_DP, N_EXPERT, TOK_DEV, D)
    cot = cotangent.reshape(N_DP, N_EXPERT, TOK_DEV, D)
    flat_routes = routes.reshape(N_DP, N_EXPERT, per_device)
    gts = gates.reshape(N_DP, N_EXPERT, TOK_DEV, ROUTED)
    places = jax.vmap(jax.vmap(slot_positions))(flat_routes)
    gate_up = w_gate_up.reshape(2, D, EXPERTS, FF).transpose(2, 0, 1, 3)
    down = w_down.reshape(EXPERTS, FF, D)

    def pack(rows, where):
        buffer = jnp.zeros((EXPERTS * CAPACITY, D), jnp.bfloat16).at[where].set(rows)
        return buffer.reshape(EXPERTS, CAPACITY, D)

    def expert_pass(items):
        inputs, grads_in, weights_up, weights_down = items
        pre = jnp.einsum('rc,gcf->grf', inputs.astype(jnp.float32), weights_up.astype(jnp.float32))
        act_in = pre[0]
        linear = pre[1]
        sig = jax.nn.sigmoid(act_in)
        hidden = (act_in * sig * linear).astype(jnp.bfloat16)
        d_hidden = jnp.dot(grads_in, weights_down.T, preferred_element_type=jnp.float32)
        d_act = (d_hidden * linear * sig * (1.0 + act_in * (1.0 - sig))).astype(jnp.bfloat16)
        d_lin = (d_hidden * act_in * sig).astype(jnp.bfloat16)
        d_pre = jnp.stack([d_act, d_lin])
        outs_sum = jnp.zeros((inputs.shape[0], D), jnp.float32)
        ins_sum = jnp.zeros((inputs.shape[0], D), jnp.float32)
        for part in range(group):
            low = part * block_width
            high = low + block_width
            outs_sum = outs_sum + round_trip(jnp.dot(hidden[:, low:high], weights_down[low:high], preferred_element_type=jnp.float32))
            ins_sum = ins_sum + round_trip(jnp.einsum('grf,gcf->rc', d_pre[:, :, low:high].astype(jnp.float32), weights_up[:, :, low:high].astype(jnp.float32)))
        grad_up = jnp.einsum('rc,grf->gcf', inputs.astype(jnp.float32), d_pre.astype(jnp.float32))
        grad_down = jnp.dot(hidden.T, grads_in, preferred_element_type=jnp.float32)
        return (outs_sum, ins_sum, round_trip(grad_up), round_trip(grad_down))

    def data_row(carry, row):
        tok_d, cot_d, place_d, gate_d = row
        token_rows = jnp.repeat(tok_d, ROUTED, axis=1)
        gate_flat = gate_d.reshape(N_EXPERT, per_device)
        cot_rows = (gate_flat[..., None] * jnp.repeat(cot_d, ROUTED, axis=1).astype(jnp.float32)).astype(jnp.bfloat16)
        send_x = jax.vmap(pack)(token_rows, place_d)
        send_y = jax.vmap(pack)(cot_rows, place_d)
        inputs = send_x.transpose(1, 0, 2, 3).reshape(EXPERTS, N_EXPERT * CAPACITY, D)
        grads_in = send_y.transpose(1, 0, 2, 3).reshape(EXPERTS, N_EXPERT * CAPACITY, D)
        outs, ins, g_up, g_down = lax.map(expert_pass, (inputs, grads_in, gate_up, down))
        outs_src = outs.reshape(EXPERTS, N_EXPERT, CAPACITY, D).transpose(1, 0, 2, 3).reshape(N_EXPERT, EXPERTS * CAPACITY, D)
        ins_src = ins.reshape(EXPERTS, N_EXPERT, CAPACITY, D).transpose(1, 0, 2, 3).reshape(N_EXPERT, EXPERTS * CAPACITY, D)
        picked_out = jax.vmap(lambda source, where: source[where])(outs_src, place_d).reshape(N_EXPERT, TOK_DEV, ROUTED, D)
        picked_in = jax.vmap(lambda source, where: source[where])(ins_src, place_d).reshape(N_EXPERT, TOK_DEV, ROUTED, D)
        row_out = lax.optimization_barrier(jnp.sum(gate_d[..., None] * picked_out, axis=2)).astype(jnp.bfloat16)
        row_in = lax.optimization_barrier(jnp.sum(picked_in, axis=2)).astype(jnp.bfloat16)
        return ((carry[0] + g_up, carry[1] + g_down), (row_out, row_in))
    start = (jnp.zeros((EXPERTS, 2, D, FF), jnp.float32), jnp.zeros((EXPERTS, FF, D), jnp.float32))
    sums, rows_out = lax.scan(data_row, start, (tok, cot, places, gts))
    sum_up = sums[0].transpose(1, 2, 0, 3).reshape(2, D, EXPERTS * FF)
    sum_down = sums[1].reshape(EXPERTS * FF, D)
    outputs = rows_out[0].reshape(TOKENS, D)
    input_grads = rows_out[1].reshape(TOKENS, D)
    new_wu, new_mu, new_vu = adam_update(w_gate_up, m_gate_up, v_gate_up, sum_up)
    new_wd, new_md, new_vd = adam_update(w_down, m_down, v_down, sum_down)
    return (outputs, input_grads, new_wu, new_mu, new_vu, new_wd, new_md, new_vd)
```

```python
import jax
import jax.numpy as jnp
from jax import lax
from jax.sharding import Mesh, PartitionSpec as P

EXPERTS = 8
CAPACITY = 20


first_decay = 0.9
second_decay = 0.95
first_correction = 1.0 - 0.9**50 * 0.9**50
second_correction = 1.0 - 0.95**50 * 0.95**50
learn_rate = 0.01
adam_epsilon = 1e-08

SWAP = [(0, 1), (1, 0)]


def slots_of(flat_routes):
    n = flat_routes.shape[0]
    onehot = (flat_routes[:, None] == jnp.arange(EXPERTS, dtype=jnp.int32)[None, :]).astype(jnp.bfloat16)
    earlier = (jnp.arange(n)[:, None] > jnp.arange(n)[None, :]).astype(jnp.bfloat16)
    before = jnp.dot(earlier, onehot, preferred_element_type=jnp.float32)
    return jnp.sum(before * onehot.astype(jnp.float32), axis=1).astype(jnp.int32)


def adam_update(weight, moment, second, grad_sum, scale):
    grad = grad_sum * scale
    moment_new = first_decay * moment + (1.0 - first_decay) * grad
    second_new = second_decay * second + (1.0 - second_decay) * grad * grad
    update = (
        moment_new / first_correction / (jnp.sqrt(second_new / second_correction) + adam_epsilon)
    )
    weight_new = (weight.astype(jnp.float32) - learn_rate * update).astype(jnp.bfloat16)
    return (weight_new, moment_new, second_new)


def dot(a, b, dims=((1,), (0,))):
    return lax.dot_general(a, b, (dims, ((), ())), preferred_element_type=jnp.float32)


def shards(
    tokens, cotangent, routes, gates, w_gate_up, w_down, m_gate_up, v_gate_up, m_down, v_down
):
    n_data, n_chip, n_core = (lax.axis_size(a) for a in ("z", "p", "c"))
    pair = n_chip // EXPERTS
    tok_rows, width = tokens.shape
    half = width // n_core
    block = n_core * CAPACITY
    hid = w_down.shape[0]
    c = lax.axis_index("c")
    orders = [
        [((z + k * n_data // n_core) % n_data) * n_core + k for z in range(n_data)]
        for k in range(n_core)
    ]

    owned = jnp.concatenate([w_gate_up[0], w_gate_up[1], w_down.T], axis=1)
    weights = lax.all_gather(owned, ("z", "c"), axis=0, tiled=True, axis_index_groups=orders)
    w_m, w_o = weights[:half], weights[half:]

    flat = routes.reshape(-1)
    place = flat * block + c * CAPACITY + slots_of(flat)
    info = jnp.concatenate([place.astype(jnp.float32)[:, None], gates], axis=1)
    info2 = jnp.concatenate([info, lax.ppermute(info, "c", SWAP)], axis=0)
    place2 = info2[:, 0].astype(jnp.int32)
    gate2 = info2[:, 1:2]
    cot = (gates * cotangent.astype(jnp.float32)).astype(jnp.bfloat16)

    def half_of(array, k):
        return lax.dynamic_slice_in_dim(array, k * half, half, axis=1)

    def both_of(k):
        return jnp.concatenate([half_of(tokens, k), half_of(cot, k)], axis=1)

    rows2 = jnp.concatenate([both_of(c), lax.ppermute(both_of(1 - c), "c", SWAP)], axis=0)
    row_id = lax.broadcasted_iota(jnp.int32, (EXPERTS, pair, block), 0) * block + (
        lax.broadcasted_iota(jnp.int32, (EXPERTS, pair, block), 2)
    )
    row_id = row_id.reshape(-1)
    pick = (row_id[:, None] == place2[None, :]).astype(jnp.bfloat16)
    packed = dot(pick, rows2).astype(jnp.bfloat16).reshape(n_chip, block, width)
    got = lax.all_to_all(packed, "p", split_axis=0, concat_axis=0, tiled=True)
    mine = got.reshape(n_chip * block, width)
    other = lax.ppermute(mine, "c", SWAP)
    x_m, y_m = mine[:, :half], mine[:, half:]
    x_o, y_o = other[:, :half], other[:, half:]

    pre = dot(x_m, w_m[:, : 2 * hid]) + dot(x_o, w_o[:, : 2 * hid])
    d_hidden = dot(y_m, w_m[:, 2 * hid :]) + dot(y_o, w_o[:, 2 * hid :])
    act_in, linear = pre[:, :hid], pre[:, hid:]
    sig = jax.nn.sigmoid(act_in)
    hidden = (act_in * sig * linear).astype(jnp.bfloat16)
    d_act = (d_hidden * linear * sig * (1.0 + act_in * (1.0 - sig))).astype(jnp.bfloat16)
    d_lin = (d_hidden * act_in * sig).astype(jnp.bfloat16)
    d_pre = jnp.concatenate([d_act, d_lin], axis=1)

    def parts(w):
        out = dot(hidden, w[:, 2 * hid :], ((1,), (1,)))
        inp = dot(d_pre, w[:, : 2 * hid], ((1,), (1,)))
        return jnp.concatenate([out.astype(jnp.bfloat16), inp.astype(jnp.bfloat16)], axis=1)

    from_other = lax.ppermute(parts(w_o), "c", SWAP)
    back = (parts(w_m).astype(jnp.float32) + from_other.astype(jnp.float32)).astype(jnp.bfloat16)

    def grads(x, y):
        up = dot(x, d_pre, ((0,), (0,))).astype(jnp.bfloat16)
        down = dot(y, hidden, ((0,), (0,))).astype(jnp.bfloat16)
        return jnp.concatenate([up, down], axis=1)

    grad = jnp.concatenate([grads(x_m, y_m), grads(x_o, y_o)], axis=0)
    grad = lax.psum_scatter(
        grad, ("z", "c"), scatter_dimension=0, tiled=True, axis_index_groups=orders
    ).astype(jnp.float32)

    back = lax.all_to_all(
        back.reshape(n_chip, block, width), "p", split_axis=0, concat_axis=0, tiled=True
    ).reshape(n_chip * block, width)
    unpick = (place2[:, None] == row_id[None, :]).astype(jnp.bfloat16)
    summed = dot(unpick, back)
    result = jnp.concatenate([summed[:, :half] * gate2, summed[:, half:]], axis=1).astype(jnp.bfloat16)
    near = result[:tok_rows]
    far = lax.ppermute(result[tok_rows:], "c", SWAP)

    def joined(cols):
        a, b = near[:, cols], far[:, cols]
        first = jnp.where(c == 0, a, b)
        second = jnp.where(c == 0, b, a)
        return jnp.concatenate([first, second], axis=1)

    outputs, input_grads = joined(slice(0, half)), joined(slice(half, width))
    scale = (tok_rows * n_data * n_chip * n_core * routes.shape[1] / EXPERTS) ** (-0.5)
    grad_up = jnp.stack([grad[:, :hid], grad[:, hid : 2 * hid]])
    new_wu, new_mu, new_vu = adam_update(w_gate_up, m_gate_up, v_gate_up, grad_up, scale)
    new_wd, new_md, new_vd = adam_update(w_down, m_down, v_down, grad[:, 2 * hid :].T, scale)
    return (outputs, input_grads, new_wu, new_mu, new_vu, new_wd, new_md, new_vd)


def solution(mesh):
    n_data, n_expert = (mesh.shape[a] for a in ("dp", "expert"))
    cores = Mesh(mesh.devices.reshape(n_data, n_expert // 2, 2), ("z", "p", "c"))
    rows = P(("z", "p", "c"), None)
    up, down = P(None, "z", ("p", "c")), P(("p", "c"), "z")
    return jax.shard_map(
        shards,
        mesh=cores,
        in_specs=(rows, rows, rows, rows, up, down, up, up, down, down),
        out_specs=(rows, rows, up, up, up, down, down, down),
        check_vma=False,
    )
```

```python
import functools

import jax
import jax.numpy as jnp
from jax import lax
from jax.experimental import pallas as pl
from jax.experimental.pallas import tpu as pltpu
from jax.sharding import Mesh, PartitionSpec as P

EXPERTS = 8
CAPACITY = 20


first_decay = 0.9
second_decay = 0.95
first_correction = 1.0 - 0.9**50 * 0.9**50
second_correction = 1.0 - 0.95**50 * 0.95**50
learn_rate = 0.01
adam_epsilon = 1e-08

SWAP = [(0, 1), (1, 0)]
BLOCKS = 2


def slots_of(flat_routes):
    n = flat_routes.shape[0]
    onehot = (flat_routes[:, None] == jnp.arange(EXPERTS, dtype=jnp.int32)[None, :]).astype(jnp.bfloat16)
    earlier = (jnp.arange(n)[:, None] > jnp.arange(n)[None, :]).astype(jnp.bfloat16)
    before = jnp.dot(earlier, onehot, preferred_element_type=jnp.float32)
    return jnp.sum(before * onehot.astype(jnp.float32), axis=1).astype(jnp.int32)


def adam_update(weight, moment, second, grad_sum, scale):
    grad = grad_sum * scale
    moment_new = first_decay * moment + (1.0 - first_decay) * grad
    second_new = second_decay * second + (1.0 - second_decay) * grad * grad
    update = (
        moment_new / first_correction / (jnp.sqrt(second_new / second_correction) + adam_epsilon)
    )
    weight_new = (weight.astype(jnp.float32) - learn_rate * update).astype(jnp.bfloat16)
    return (weight_new, moment_new, second_new)


def dot(a, b, dims=((1,), (0,))):
    return lax.dot_general(a, b, (dims, ((), ())), preferred_element_type=jnp.float32)


MIB = 1 << 20


def call(body, grid, in_specs, out_specs, out_shape, flops, scratch=(), vmem=40):
    return pl.pallas_call(
        body,
        grid=(grid,),
        in_specs=in_specs,
        out_specs=out_specs,
        out_shape=out_shape,
        scratch_shapes=list(scratch),
        compiler_params=pltpu.CompilerParams(vmem_limit_bytes=vmem * MIB),
        cost_estimate=pl.CostEstimate(flops=flops, bytes_accessed=12 * MIB, transcendentals=0),
    )


def pre_body(hid, x_ref, y_ref, w_ref, acc_ref):
    @pl.when(pl.program_id(0) == 0)
    def _():
        acc_ref[...] = jnp.zeros_like(acc_ref)

    acc_ref[:, : 2 * hid] += dot(x_ref[...], w_ref[:, : 2 * hid])
    acc_ref[:, 2 * hid :] += dot(y_ref[...], w_ref[:, 2 * hid :])


def first_half(rows, weights, hid, blocks):
    n, width = rows.shape
    cols = width // 2 // blocks
    return call(
        functools.partial(pre_body, hid),
        blocks,
        [
            pl.BlockSpec((n, cols), lambda i: (0, i)),
            pl.BlockSpec((n, cols), lambda i: (0, blocks + i)),
            pl.BlockSpec((cols, 3 * hid), lambda i: (i, 0)),
        ],
        pl.BlockSpec((n, 3 * hid), lambda i: (0, 0)),
        jax.ShapeDtypeStruct((n, 3 * hid), jnp.float32),
        flops=3 * n * width * hid,
    )(rows, rows, weights)


def mid_body(hid, blocks, pre_ref, x_ref, y_ref, w_ref, part_ref, deriv_ref, acc_ref):
    step = pl.program_id(0)

    @pl.when(step == 0)
    def _():
        acc_ref[...] = pre_ref[...]

    @pl.when(step < blocks)
    def _():
        acc_ref[:, : 2 * hid] += dot(x_ref[...], w_ref[:, : 2 * hid])
        acc_ref[:, 2 * hid :] += dot(y_ref[...], w_ref[:, 2 * hid :])

    @pl.when(step == blocks - 1)
    def _():
        act, linear, d_hidden = (acc_ref[:, k * hid : (k + 1) * hid] for k in range(3))
        sig = jax.nn.sigmoid(act)
        gated = act * sig
        deriv_ref[:, :hid] = (d_hidden * linear * sig * (1.0 + act * (1.0 - sig))).astype(jnp.bfloat16)
        deriv_ref[:, hid : 2 * hid] = (d_hidden * gated).astype(jnp.bfloat16)
        deriv_ref[:, 2 * hid :] = (gated * linear).astype(jnp.bfloat16)

    @pl.when((step >= blocks) & (step < 2 * blocks))
    def _():
        part_ref[...] = dot(deriv_ref[:, 2 * hid :], w_ref[:, 2 * hid :], ((1,), (1,))).astype(jnp.bfloat16)

    @pl.when(step >= 2 * blocks)
    def _():
        part_ref[...] = dot(deriv_ref[:, : 2 * hid], w_ref[:, : 2 * hid], ((1,), (1,))).astype(jnp.bfloat16)


def second_half(pre, rows, weights, hid, blocks):
    n, width = rows.shape
    cols = width // 2 // blocks
    start = weights.shape[0] // cols - blocks

    def reading(i):
        return jnp.minimum(i, blocks - 1)

    return call(
        functools.partial(mid_body, hid, blocks),
        3 * blocks,
        [
            pl.BlockSpec((n, 3 * hid), lambda i: (0, 0)),
            pl.BlockSpec((n, cols), lambda i: (0, reading(i))),
            pl.BlockSpec((n, cols), lambda i: (0, blocks + reading(i))),
            pl.BlockSpec((cols, 3 * hid), lambda i: (start + lax.rem(i, blocks), 0)),
        ],
        [
            pl.BlockSpec((n, cols), lambda i: (0, jnp.maximum(i - blocks, 0))),
            pl.BlockSpec((n, 3 * hid), lambda i: (0, 0)),
        ],
        [
            jax.ShapeDtypeStruct((n, width), jnp.bfloat16),
            jax.ShapeDtypeStruct((n, 3 * hid), jnp.bfloat16),
        ],
        flops=6 * n * width * hid,
        scratch=[pltpu.VMEM((n, 3 * hid), jnp.float32)],
    )(pre, rows, rows, weights)


def grad_body(hid, blocks, xm_ref, ym_ref, xo_ref, yo_ref, deriv_ref, grad_ref):
    def write(x, y):
        grad_ref[:, : 2 * hid] = dot(x, deriv_ref[:, : 2 * hid], ((0,), (0,))).astype(jnp.bfloat16)
        grad_ref[:, 2 * hid :] = dot(y, deriv_ref[:, 2 * hid :], ((0,), (0,))).astype(jnp.bfloat16)

    @pl.when(pl.program_id(0) < blocks)
    def _():
        write(xm_ref[...], ym_ref[...])

    @pl.when(pl.program_id(0) >= blocks)
    def _():
        write(xo_ref[...], yo_ref[...])


def weight_grads(mine, other, deriv, hid, blocks):
    n, width = mine.shape
    cols = width // 2 // blocks

    def early(i):
        return jnp.minimum(i, blocks - 1)

    def late(i):
        return jnp.maximum(i - blocks, 0)

    return call(
        functools.partial(grad_body, hid, blocks),
        2 * blocks,
        [
            pl.BlockSpec((n, cols), lambda i: (0, early(i))),
            pl.BlockSpec((n, cols), lambda i: (0, blocks + early(i))),
            pl.BlockSpec((n, cols), lambda i: (0, late(i))),
            pl.BlockSpec((n, cols), lambda i: (0, blocks + late(i))),
            pl.BlockSpec((n, 3 * hid), lambda i: (0, 0)),
        ],
        pl.BlockSpec((cols, 3 * hid), lambda i: (i, 0)),
        jax.ShapeDtypeStruct((width, 3 * hid), jnp.bfloat16),
        flops=6 * n * width * hid,
    )(mine, mine, other, other, deriv)


def back_body(hid, blocks, deriv_ref, w_ref, other_ref, back_ref):
    def write(part):
        back_ref[...] = (part + other_ref[...].astype(jnp.float32)).astype(jnp.bfloat16)

    @pl.when(pl.program_id(0) < blocks)
    def _():
        write(dot(deriv_ref[:, 2 * hid :], w_ref[:, 2 * hid :], ((1,), (1,))))

    @pl.when(pl.program_id(0) >= blocks)
    def _():
        write(dot(deriv_ref[:, : 2 * hid], w_ref[:, : 2 * hid], ((1,), (1,))))


def sent_back(deriv, weights, from_other, hid, blocks):
    n, width = from_other.shape
    cols = width // 2 // blocks
    return call(
        functools.partial(back_body, hid, blocks),
        2 * blocks,
        [
            pl.BlockSpec((n, 3 * hid), lambda i: (0, 0)),
            pl.BlockSpec((cols, 3 * hid), lambda i: (lax.rem(i, blocks), 0)),
            pl.BlockSpec((n, cols), lambda i: (0, i)),
        ],
        pl.BlockSpec((n, cols), lambda i: (0, i)),
        jax.ShapeDtypeStruct((n, width), jnp.bfloat16),
        flops=3 * n * width * hid,
    )(deriv, weights, from_other)


def shards(
    tokens, cotangent, routes, gates, w_gate_up, w_down, m_gate_up, v_gate_up, m_down, v_down
):
    n_data, n_chip, n_core = (lax.axis_size(a) for a in ("z", "p", "c"))
    pair = n_chip // EXPERTS
    tok_rows, width = tokens.shape
    half = width // n_core
    block = n_core * CAPACITY
    hid = w_down.shape[0]
    c = lax.axis_index("c")
    orders = [
        [((z + k * n_data // n_core) % n_data) * n_core + k for z in range(n_data)]
        for k in range(n_core)
    ]

    owned = jnp.concatenate([w_gate_up[0], w_gate_up[1], w_down.T], axis=1)
    weights = lax.all_gather(owned, ("z", "c"), axis=0, tiled=True, axis_index_groups=orders)

    flat = routes.reshape(-1)
    place = flat * block + c * CAPACITY + slots_of(flat)
    info = jnp.concatenate([place.astype(jnp.float32)[:, None], gates], axis=1)
    info2 = jnp.concatenate([info, lax.ppermute(info, "c", SWAP)], axis=0)
    place2 = info2[:, 0].astype(jnp.int32)
    gate2 = info2[:, 1:2]
    cot = (gates * cotangent.astype(jnp.float32)).astype(jnp.bfloat16)

    def half_of(array, k):
        return lax.dynamic_slice_in_dim(array, k * half, half, axis=1)

    def both_of(k):
        return jnp.concatenate([half_of(tokens, k), half_of(cot, k)], axis=1)

    rows2 = jnp.concatenate([both_of(c), lax.ppermute(both_of(1 - c), "c", SWAP)], axis=0)
    row_id = lax.broadcasted_iota(jnp.int32, (EXPERTS, pair, block), 0) * block + (
        lax.broadcasted_iota(jnp.int32, (EXPERTS, pair, block), 2)
    )
    row_id = row_id.reshape(-1)
    pick = (row_id[:, None] == place2[None, :]).astype(jnp.bfloat16)
    packed = dot(pick, rows2).astype(jnp.bfloat16).reshape(n_chip, block, width)
    got = lax.all_to_all(packed, "p", split_axis=0, concat_axis=0, tiled=True)
    mine = got.reshape(n_chip * block, width)
    other = lax.ppermute(mine, "c", SWAP)

    pre = first_half(mine, weights, hid, BLOCKS)
    parts_o, deriv = second_half(pre, other, weights, hid, BLOCKS)
    from_other = lax.ppermute(parts_o, "c", SWAP)
    grad = weight_grads(mine, other, deriv, hid, BLOCKS)
    grad = lax.psum_scatter(
        grad, ("z", "c"), scatter_dimension=0, tiled=True, axis_index_groups=orders
    ).astype(jnp.float32)

    back = sent_back(deriv, weights, from_other, hid, BLOCKS)
    back = lax.all_to_all(
        back.reshape(n_chip, block, width), "p", split_axis=0, concat_axis=0, tiled=True
    ).reshape(n_chip * block, width)
    unpick = (place2[:, None] == row_id[None, :]).astype(jnp.bfloat16)
    summed = dot(unpick, back)
    result = jnp.concatenate([summed[:, :half] * gate2, summed[:, half:]], axis=1).astype(jnp.bfloat16)
    near = result[:tok_rows]
    far = lax.ppermute(result[tok_rows:], "c", SWAP)

    def joined(cols):
        a, b = near[:, cols], far[:, cols]
        first = jnp.where(c == 0, a, b)
        second = jnp.where(c == 0, b, a)
        return jnp.concatenate([first, second], axis=1)

    outputs, input_grads = joined(slice(0, half)), joined(slice(half, width))
    scale = (tok_rows * n_data * n_chip * n_core * routes.shape[1] / EXPERTS) ** (-0.5)
    grad_up = jnp.stack([grad[:, :hid], grad[:, hid : 2 * hid]])
    new_wu, new_mu, new_vu = adam_update(w_gate_up, m_gate_up, v_gate_up, grad_up, scale)
    new_wd, new_md, new_vd = adam_update(w_down, m_down, v_down, grad[:, 2 * hid :].T, scale)
    return (outputs, input_grads, new_wu, new_mu, new_vu, new_wd, new_md, new_vd)


def solution(mesh):
    n_data, n_expert = (mesh.shape[a] for a in ("dp", "expert"))
    cores = Mesh(mesh.devices.reshape(n_data, n_expert // 2, 2), ("z", "p", "c"))
    rows = P(("z", "p", "c"), None)
    up, down = P(None, "z", ("p", "c")), P(("p", "c"), "z")
    return jax.shard_map(
        shards,
        mesh=cores,
        in_specs=(rows, rows, rows, rows, up, down, up, up, down, down),
        out_specs=(rows, rows, up, up, up, down, down, down),
        check_vma=False,
    )
```

```python
import functools

import jax
import jax.numpy as jnp
from jax import lax
from jax.experimental import pallas as pl
from jax.experimental.pallas import tpu as pltpu
from jax.sharding import Mesh, PartitionSpec as P

EXPERTS = 8
CAPACITY = 20


first_decay = 0.9
second_decay = 0.95
first_correction = 1.0 - 0.9**50 * 0.9**50
second_correction = 1.0 - 0.95**50 * 0.95**50
learn_rate = 0.01
adam_epsilon = 1e-08

SWAP = [(0, 1), (1, 0)]
BLOCKS = 2


def slots_of(flat_routes):
    n = flat_routes.shape[0]
    onehot = (flat_routes[:, None] == jnp.arange(EXPERTS, dtype=jnp.int32)[None, :]).astype(jnp.bfloat16)
    earlier = (jnp.arange(n)[:, None] > jnp.arange(n)[None, :]).astype(jnp.bfloat16)
    before = jnp.dot(earlier, onehot, preferred_element_type=jnp.float32)
    return jnp.sum(before * onehot.astype(jnp.float32), axis=1).astype(jnp.int32)


def adam_update(weight, moment, second, grad_sum, scale):
    grad = grad_sum * scale
    moment_new = first_decay * moment + (1.0 - first_decay) * grad
    second_new = second_decay * second + (1.0 - second_decay) * grad * grad
    update = (
        moment_new / first_correction / (jnp.sqrt(second_new / second_correction) + adam_epsilon)
    )
    weight_new = (weight.astype(jnp.float32) - learn_rate * update).astype(jnp.bfloat16)
    return (weight_new, moment_new, second_new)


def dot(a, b, dims=((1,), (0,))):
    return lax.dot_general(a, b, (dims, ((), ())), preferred_element_type=jnp.float32)


MIB = 1 << 20
VMEM = 57


def call(body, grid, in_specs, out_specs, out_shape, flops, scratch=(), vmem=VMEM):
    return pl.pallas_call(
        body,
        grid=(grid,),
        in_specs=in_specs,
        out_specs=out_specs,
        out_shape=out_shape,
        scratch_shapes=list(scratch),
        compiler_params=pltpu.CompilerParams(vmem_limit_bytes=vmem * MIB),
        cost_estimate=pl.CostEstimate(flops=flops, bytes_accessed=12 * MIB, transcendentals=0),
    )


def pre_body(hid, x_ref, y_ref, w_ref, acc_ref):
    @pl.when(pl.program_id(0) == 0)
    def _():
        acc_ref[...] = jnp.zeros_like(acc_ref)

    acc_ref[:, : 2 * hid] += dot(x_ref[...], w_ref[:, : 2 * hid])
    acc_ref[:, 2 * hid :] += dot(y_ref[...], w_ref[:, 2 * hid :])


def first_half(rows, weights, hid, blocks):
    n, width = rows.shape
    cols = width // 2 // blocks
    return call(
        functools.partial(pre_body, hid),
        blocks,
        [
            pl.BlockSpec((n, cols), lambda i: (0, i)),
            pl.BlockSpec((n, cols), lambda i: (0, blocks + i)),
            pl.BlockSpec((cols, 3 * hid), lambda i: (i, 0)),
        ],
        pl.BlockSpec((n, 3 * hid), lambda i: (0, 0)),
        jax.ShapeDtypeStruct((n, 3 * hid), jnp.float32),
        flops=3 * n * width * hid,
    )(rows, rows, weights)


def mid_body(hid, blocks, pre_ref, x_ref, y_ref, w_ref, deriv_ref, acc_ref):
    step = pl.program_id(0)

    @pl.when(step == 0)
    def _():
        acc_ref[...] = pre_ref[...]

    acc_ref[:, : 2 * hid] += dot(x_ref[...], w_ref[:, : 2 * hid])
    acc_ref[:, 2 * hid :] += dot(y_ref[...], w_ref[:, 2 * hid :])

    @pl.when(step == blocks - 1)
    def _():
        act, linear, d_hidden = (acc_ref[:, k * hid : (k + 1) * hid] for k in range(3))
        sig = jax.nn.sigmoid(act)
        gated = act * sig
        deriv_ref[:, :hid] = (d_hidden * linear * sig * (1.0 + act * (1.0 - sig))).astype(jnp.bfloat16)
        deriv_ref[:, hid : 2 * hid] = (d_hidden * gated).astype(jnp.bfloat16)
        deriv_ref[:, 2 * hid :] = (gated * linear).astype(jnp.bfloat16)


def second_half(pre, rows, weights, hid, blocks):
    n, width = rows.shape
    cols = width // 2 // blocks
    return call(
        functools.partial(mid_body, hid, blocks),
        blocks,
        [
            pl.BlockSpec((n, 3 * hid), lambda i: (0, 0)),
            pl.BlockSpec((n, cols), lambda i: (0, i)),
            pl.BlockSpec((n, cols), lambda i: (0, blocks + i)),
            pl.BlockSpec((cols, 3 * hid), lambda i: (blocks + i, 0)),
        ],
        pl.BlockSpec((n, 3 * hid), lambda i: (0, 0)),
        jax.ShapeDtypeStruct((n, 3 * hid), jnp.bfloat16),
        flops=3 * n * width * hid,
        scratch=[pltpu.VMEM((n, 3 * hid), jnp.float32)],
    )(pre, rows, rows, weights)


def grad_body(hid, blocks, xm_ref, ym_ref, xo_ref, yo_ref, deriv_ref, grad_ref):
    def write(x, y):
        grad_ref[:, : 2 * hid] = dot(x, deriv_ref[:, : 2 * hid], ((0,), (0,))).astype(jnp.bfloat16)
        grad_ref[:, 2 * hid :] = dot(y, deriv_ref[:, 2 * hid :], ((0,), (0,))).astype(jnp.bfloat16)

    @pl.when(pl.program_id(0) < blocks)
    def _():
        write(xm_ref[...], ym_ref[...])

    @pl.when(pl.program_id(0) >= blocks)
    def _():
        write(xo_ref[...], yo_ref[...])


def weight_grads(mine, other, deriv, hid, blocks):
    n, width = mine.shape
    cols = width // 2 // blocks

    def early(i):
        return jnp.minimum(i, blocks - 1)

    def late(i):
        return jnp.maximum(i - blocks, 0)

    return call(
        functools.partial(grad_body, hid, blocks),
        2 * blocks,
        [
            pl.BlockSpec((n, cols), lambda i: (0, early(i))),
            pl.BlockSpec((n, cols), lambda i: (0, blocks + early(i))),
            pl.BlockSpec((n, cols), lambda i: (0, late(i))),
            pl.BlockSpec((n, cols), lambda i: (0, blocks + late(i))),
            pl.BlockSpec((n, 3 * hid), lambda i: (0, 0)),
        ],
        pl.BlockSpec((cols, 3 * hid), lambda i: (i, 0)),
        jax.ShapeDtypeStruct((width, 3 * hid), jnp.bfloat16),
        flops=6 * n * width * hid,
    )(mine, mine, other, other, deriv)


def back_body(hid, blocks, deriv_m_ref, deriv_o_ref, w_m_ref, w_o_ref, back_ref):
    def write(cols):
        mine = dot(deriv_m_ref[:, cols], w_m_ref[:, cols], ((1,), (1,)))
        other = dot(deriv_o_ref[:, cols], w_o_ref[:, cols], ((1,), (1,)))
        back_ref[...] = (mine + other).astype(jnp.bfloat16)

    @pl.when(pl.program_id(0) < blocks)
    def _():
        write(slice(2 * hid, 3 * hid))

    @pl.when(pl.program_id(0) >= blocks)
    def _():
        write(slice(0, 2 * hid))


def sent_back(deriv_m, deriv_o, w_m, w_o, hid, blocks):
    n = deriv_m.shape[0]
    cols = w_o.shape[0] // blocks
    deriv = pl.BlockSpec((n, 3 * hid), lambda i: (0, 0))
    weight = pl.BlockSpec((cols, 3 * hid), lambda i: (lax.rem(i, blocks), 0))
    return call(
        functools.partial(back_body, hid, blocks),
        2 * blocks,
        [deriv, deriv, weight, weight],
        pl.BlockSpec((n, cols), lambda i: (0, i)),
        jax.ShapeDtypeStruct((n, 2 * w_o.shape[0]), jnp.bfloat16),
        flops=12 * n * w_o.shape[0] * hid,
    )(deriv_m, deriv_o, w_m, w_o)


def unpack_body(pick_ref, gate_ref, back_ref, near_ref, far_ref):
    n = near_ref.shape[0]
    picked = dot(pick_ref[...], back_ref[...])
    picked = picked * jnp.where(pl.program_id(0) == 0, gate_ref[...], 1.0)
    near_ref[...] = picked[:n].astype(jnp.bfloat16)
    far_ref[...] = picked[n:].astype(jnp.bfloat16)


def unpacked(pick, gate, back):
    tokens, rows = pick.shape
    half = back.shape[1] // 2
    result = pl.BlockSpec((tokens // 2, half), lambda i: (0, i))
    shape = jax.ShapeDtypeStruct((tokens // 2, 2 * half), jnp.bfloat16)
    return call(
        unpack_body,
        2,
        [
            pl.BlockSpec((tokens, rows), lambda i: (0, 0)),
            pl.BlockSpec((tokens, 1), lambda i: (0, 0)),
            pl.BlockSpec((rows, half), lambda i: (0, i)),
        ],
        [result, result],
        [shape, shape],
        flops=4 * tokens * rows * half,
    )(pick, gate, back)


def join_body(core_ref, near_ref, far_ref, out_ref, grad_ref):
    half = near_ref.shape[1] // 2
    first = core_ref[0] == 0
    for ref, cols in ((out_ref, slice(0, half)), (grad_ref, slice(half, 2 * half))):
        near, far = near_ref[:, cols], far_ref[:, cols]
        ref[:, :half] = jnp.where(first, near, far)
        ref[:, half:] = jnp.where(first, far, near)


def joined(core, near, far):
    whole = pl.BlockSpec(near.shape, lambda i: (0, 0))
    shape = jax.ShapeDtypeStruct(near.shape, jnp.bfloat16)
    return call(
        join_body,
        1,
        [pl.BlockSpec(memory_space=pltpu.SMEM), whole, whole],
        [whole, whole],
        [shape, shape],
        flops=near.size,
    )(core.reshape(1), near, far)


def shards(
    tokens, cotangent, routes, gates, w_gate_up, w_down, m_gate_up, v_gate_up, m_down, v_down
):
    n_data, n_chip, n_core = (lax.axis_size(a) for a in ("z", "p", "c"))
    pair = n_chip // EXPERTS
    tok_rows, width = tokens.shape
    half = width // n_core
    block = n_core * CAPACITY
    hid = w_down.shape[0]
    c = lax.axis_index("c")
    orders = [
        [((z + k * n_data // n_core) % n_data) * n_core + k for z in range(n_data)]
        for k in range(n_core)
    ]

    owned = jnp.concatenate([w_gate_up[0], w_gate_up[1], w_down.T], axis=1)
    weights = lax.all_gather(owned, ("z", "c"), axis=0, tiled=True, axis_index_groups=orders)

    flat = routes.reshape(-1)
    place = flat * block + c * CAPACITY + slots_of(flat)
    info = jnp.concatenate([place.astype(jnp.float32)[:, None], gates], axis=1)
    info2 = jnp.concatenate([info, lax.ppermute(info, "c", SWAP)], axis=0)
    place2 = info2[:, 0].astype(jnp.int32)
    gate2 = info2[:, 1:2]
    cot = (gates * cotangent.astype(jnp.float32)).astype(jnp.bfloat16)

    def half_of(array, k):
        return lax.dynamic_slice_in_dim(array, k * half, half, axis=1)

    def both_of(k):
        return jnp.concatenate([half_of(tokens, k), half_of(cot, k)], axis=1)

    rows2 = jnp.concatenate([both_of(c), lax.ppermute(both_of(1 - c), "c", SWAP)], axis=0)
    row_id = lax.broadcasted_iota(jnp.int32, (EXPERTS, pair, block), 0) * block + (
        lax.broadcasted_iota(jnp.int32, (EXPERTS, pair, block), 2)
    )
    row_id = row_id.reshape(-1)
    pick = (row_id[:, None] == place2[None, :]).astype(jnp.bfloat16)
    packed = dot(pick, rows2).astype(jnp.bfloat16).reshape(n_chip, block, width)
    got = lax.all_to_all(packed, "p", split_axis=0, concat_axis=0, tiled=True)
    mine = got.reshape(n_chip * block, width)
    other = lax.ppermute(mine, "c", SWAP)

    weights_o = lax.ppermute(weights[half:], "c", SWAP)
    pre = first_half(mine, weights, hid, BLOCKS)
    deriv = second_half(pre, other, weights, hid, BLOCKS)
    deriv, weights_o = lax.optimization_barrier((deriv, weights_o))
    deriv_o = lax.ppermute(deriv, "c", SWAP)
    grad = weight_grads(mine, other, deriv, hid, BLOCKS)
    grad, deriv_o = lax.optimization_barrier((grad, deriv_o))
    grad = lax.psum_scatter(
        grad, ("z", "c"), scatter_dimension=0, tiled=True, axis_index_groups=orders
    ).astype(jnp.float32)

    back = sent_back(deriv, deriv_o, weights, weights_o, hid, BLOCKS)
    back = lax.all_to_all(
        back.reshape(n_chip, block, width), "p", split_axis=0, concat_axis=0, tiled=True
    ).reshape(n_chip * block, width)
    unpick = (place2[:, None] == row_id[None, :]).astype(jnp.bfloat16)
    near, far = unpacked(unpick, gate2, back)
    far = lax.ppermute(far, "c", SWAP)
    scale = (tok_rows * n_data * n_chip * n_core * routes.shape[1] / EXPERTS) ** (-0.5)
    grad_up = jnp.stack([grad[:, :hid], grad[:, hid : 2 * hid]])
    new_wu, new_mu, new_vu = adam_update(w_gate_up, m_gate_up, v_gate_up, grad_up, scale)
    new_wd, new_md, new_vd = adam_update(w_down, m_down, v_down, grad[:, 2 * hid :].T, scale)
    far, new_mu = lax.optimization_barrier((far, new_mu))
    outputs, input_grads = joined(c, near, far)
    return (outputs, input_grads, new_wu, new_mu, new_vu, new_wd, new_md, new_vd)


def solution(mesh):
    n_data, n_expert = (mesh.shape[a] for a in ("dp", "expert"))
    cores = Mesh(mesh.devices.reshape(n_data, n_expert // 2, 2), ("z", "p", "c"))
    rows = P(("z", "p", "c"), None)
    up, down = P(None, "z", ("p", "c")), P(("p", "c"), "z")
    return jax.shard_map(
        shards,
        mesh=cores,
        in_specs=(rows, rows, rows, rows, up, down, up, up, down, down),
        out_specs=(rows, rows, up, up, up, down, down, down),
        check_vma=False,
    )
```

```python
import functools

import jax
import jax.numpy as jnp
from jax import lax
from jax.experimental import pallas as pl
from jax.experimental.pallas import tpu as pltpu
from jax.sharding import Mesh, PartitionSpec as P

EXPERTS = 8
CAPACITY = 20


first_decay = 0.9
second_decay = 0.95
first_correction = 1.0 - 0.9**50 * 0.9**50
second_correction = 1.0 - 0.95**50 * 0.95**50
learn_rate = 0.01
adam_epsilon = 1e-08

SWAP = [(0, 1), (1, 0)]
BLOCKS = 2


def slots_of(flat_routes):
    n = flat_routes.shape[0]
    onehot = (flat_routes[:, None] == jnp.arange(EXPERTS, dtype=jnp.int32)[None, :]).astype(jnp.bfloat16)
    earlier = (jnp.arange(n)[:, None] > jnp.arange(n)[None, :]).astype(jnp.bfloat16)
    before = jnp.dot(earlier, onehot, preferred_element_type=jnp.float32)
    return jnp.sum(before * onehot.astype(jnp.float32), axis=1).astype(jnp.int32)


def adam_update(weight, moment, second, grad_sum, scale):
    grad = grad_sum * scale
    moment_new = first_decay * moment + (1.0 - first_decay) * grad
    second_new = second_decay * second + (1.0 - second_decay) * grad * grad
    update = (
        moment_new / first_correction / (jnp.sqrt(second_new / second_correction) + adam_epsilon)
    )
    weight_new = (weight.astype(jnp.float32) - learn_rate * update).astype(jnp.bfloat16)
    return (weight_new, moment_new, second_new)


def dot(a, b, dims=((1,), (0,))):
    return lax.dot_general(a, b, (dims, ((), ())), preferred_element_type=jnp.float32)


MIB = 1 << 20
VMEM = 56
BACK_VMEM = 40
GRAD_VMEM = 56
LANES = 128


def call(body, grid, in_specs, out_specs, out_shape, flops, scratch=(), vmem=VMEM):
    return pl.pallas_call(
        body,
        grid=(grid,),
        in_specs=in_specs,
        out_specs=out_specs,
        out_shape=out_shape,
        scratch_shapes=list(scratch),
        compiler_params=pltpu.CompilerParams(vmem_limit_bytes=vmem * MIB),
        cost_estimate=pl.CostEstimate(flops=flops, bytes_accessed=12 * MIB, transcendentals=0),
    )


def pre_body(hid, x_ref, y_ref, w_ref, acc_ref):
    @pl.when(pl.program_id(0) == 0)
    def _():
        acc_ref[...] = jnp.zeros_like(acc_ref)

    acc_ref[:, : 2 * hid] += dot(x_ref[...], w_ref[:, : 2 * hid])
    acc_ref[:, 2 * hid :] += dot(y_ref[...], w_ref[:, 2 * hid :])


def first_half(rows, weights, hid, blocks):
    n, width = rows.shape
    cols = width // 2 // blocks
    return call(
        functools.partial(pre_body, hid),
        blocks,
        [
            pl.BlockSpec((n, cols), lambda i: (0, i)),
            pl.BlockSpec((n, cols), lambda i: (0, blocks + i)),
            pl.BlockSpec((cols, 3 * hid), lambda i: (i, 0)),
        ],
        pl.BlockSpec((n, 3 * hid), lambda i: (0, 0)),
        jax.ShapeDtypeStruct((n, 3 * hid), jnp.float32),
        flops=3 * n * width * hid,
    )(rows, rows, weights)


def write_grads(hid, x, y, deriv_ref, grad_ref):
    grad_ref[:, : 2 * hid] = dot(x, deriv_ref[:, : 2 * hid], ((0,), (0,))).astype(jnp.bfloat16)
    grad_ref[:, 2 * hid :] = dot(y, deriv_ref[:, 2 * hid :], ((0,), (0,))).astype(jnp.bfloat16)


def mid_body(hid, blocks, pre_ref, x_ref, y_ref, w_ref, deriv_ref, grad_ref, acc_ref):
    step = pl.program_id(0)

    @pl.when(step == 0)
    def _():
        acc_ref[...] = pre_ref[...]

    @pl.when(step < blocks)
    def _():
        acc_ref[:, : 2 * hid] += dot(x_ref[...], w_ref[:, : 2 * hid])
        acc_ref[:, 2 * hid :] += dot(y_ref[...], w_ref[:, 2 * hid :])

    @pl.when(step == blocks - 1)
    def _():
        act, linear, d_hidden = (acc_ref[:, k * hid : (k + 1) * hid] for k in range(3))
        sig = jax.nn.sigmoid(act)
        gated = act * sig
        deriv_ref[:, :hid] = (d_hidden * linear * sig * (1.0 + act * (1.0 - sig))).astype(jnp.bfloat16)
        deriv_ref[:, hid : 2 * hid] = (d_hidden * gated).astype(jnp.bfloat16)
        deriv_ref[:, 2 * hid :] = (gated * linear).astype(jnp.bfloat16)

    @pl.when(step >= blocks)
    def _():
        write_grads(hid, x_ref[...], y_ref[...], deriv_ref, grad_ref)


def second_half(pre, rows, weights, hid, blocks):
    n, width = rows.shape
    cols = width // 2 // blocks

    def at(i):
        return jnp.minimum(i, 2 * blocks - 1 - i)

    return call(
        functools.partial(mid_body, hid, blocks),
        2 * blocks,
        [
            pl.BlockSpec((n, 3 * hid), lambda i: (0, 0)),
            pl.BlockSpec((n, cols), lambda i: (0, at(i))),
            pl.BlockSpec((n, cols), lambda i: (0, blocks + at(i))),
            pl.BlockSpec((cols, 3 * hid), lambda i: (blocks + jnp.minimum(i, blocks - 1), 0)),
        ],
        [
            pl.BlockSpec((n, 3 * hid), lambda i: (0, 0)),
            pl.BlockSpec((cols, 3 * hid), lambda i: (blocks + jnp.minimum(blocks - 1, 2 * blocks - 1 - i), 0)),
        ],
        [
            jax.ShapeDtypeStruct((n, 3 * hid), jnp.bfloat16),
            jax.ShapeDtypeStruct((width, 3 * hid), jnp.bfloat16),
        ],
        flops=6 * n * width * hid,
        scratch=[pltpu.VMEM((n, 3 * hid), jnp.float32)],
    )(pre, rows, rows, weights)


def grad_body(hid, x_ref, y_ref, deriv_ref, _, grad_ref):
    write_grads(hid, x_ref[...], y_ref[...], deriv_ref, grad_ref)


def first_grads(rows, deriv, grad, hid, blocks):
    n, width = rows.shape
    cols = width // 2 // blocks
    return pl.pallas_call(
        functools.partial(grad_body, hid),
        grid=(blocks,),
        in_specs=[
            pl.BlockSpec((n, cols), lambda i: (0, i)),
            pl.BlockSpec((n, cols), lambda i: (0, blocks + i)),
            pl.BlockSpec((n, 3 * hid), lambda i: (0, 0)),
            pl.BlockSpec(memory_space=pl.ANY),
        ],
        out_specs=pl.BlockSpec((cols, 3 * hid), lambda i: (i, 0)),
        out_shape=jax.ShapeDtypeStruct((width, 3 * hid), jnp.bfloat16),
        input_output_aliases={3: 0},
        compiler_params=pltpu.CompilerParams(vmem_limit_bytes=GRAD_VMEM * MIB),
        cost_estimate=pl.CostEstimate(flops=3 * n * width * hid, bytes_accessed=12 * MIB, transcendentals=0),
    )(rows, rows, deriv, grad)


def back_body(hid, deriv_m_ref, deriv_o_ref, w_m_ref, w_o_ref, back_ref):
    def write(cols):
        mine = dot(deriv_m_ref[:, cols], w_m_ref[:, cols], ((1,), (1,)))
        other = dot(deriv_o_ref[:, cols], w_o_ref[:, cols], ((1,), (1,)))
        back_ref[...] = (mine + other).astype(jnp.bfloat16)

    @pl.when(lax.rem(pl.program_id(0), 2) == 0)
    def _():
        write(slice(2 * hid, 3 * hid))

    @pl.when(lax.rem(pl.program_id(0), 2) == 1)
    def _():
        write(slice(0, 2 * hid))


def sent_back(deriv_m, deriv_o, w_m, w_o, hid, blocks):
    n = deriv_m.shape[0]
    cols = w_o.shape[0] // blocks
    deriv = pl.BlockSpec((n, 3 * hid), lambda i: (0, 0))
    weight = pl.BlockSpec((cols, 3 * hid), lambda i: (lax.div(i, 2), 0))
    return call(
        functools.partial(back_body, hid),
        2 * blocks,
        [deriv, deriv, weight, weight],
        pl.BlockSpec((n, cols), lambda i: (0, lax.div(i, 2) + blocks * lax.rem(i, 2))),
        jax.ShapeDtypeStruct((n, 2 * w_o.shape[0]), jnp.bfloat16),
        flops=12 * n * w_o.shape[0] * hid,
        vmem=BACK_VMEM,
    )(deriv_m, deriv_o, w_m, w_o)


def unpack_body(pick_ref, gate_ref, back_ref, near_ref, far_ref):
    n = near_ref.shape[0]
    picked = dot(pick_ref[...], back_ref[...])
    picked = picked * jnp.where(pl.program_id(0) == 0, gate_ref[:, :1], 1.0)
    near_ref[...] = picked[:n].astype(jnp.bfloat16)
    far_ref[...] = picked[n:].astype(jnp.bfloat16)


def unpacked(pick, gate, back):
    tokens, rows = pick.shape
    half = back.shape[1] // 2
    result = pl.BlockSpec((tokens // 2, half), lambda i: (0, i))
    shape = jax.ShapeDtypeStruct((tokens // 2, 2 * half), jnp.bfloat16)
    return call(
        unpack_body,
        2,
        [
            pl.BlockSpec((tokens, rows), lambda i: (0, 0)),
            pl.BlockSpec((tokens, LANES), lambda i: (0, 0)),
            pl.BlockSpec((rows, half), lambda i: (0, i)),
        ],
        [result, result],
        [shape, shape],
        flops=4 * tokens * rows * half,
        vmem=20,
    )(pick, gate, back)


def join_body(core_ref, near_ref, far_ref, out_ref, grad_ref):
    half = near_ref.shape[1] // 2
    first = core_ref[0] == 0
    for ref, cols in ((out_ref, slice(0, half)), (grad_ref, slice(half, 2 * half))):
        near, far = near_ref[:, cols], far_ref[:, cols]
        ref[:, :half] = jnp.where(first, near, far)
        ref[:, half:] = jnp.where(first, far, near)


def joined(core, near, far):
    whole = pl.BlockSpec(near.shape, lambda i: (0, 0))
    shape = jax.ShapeDtypeStruct(near.shape, jnp.bfloat16)
    return call(
        join_body,
        1,
        [pl.BlockSpec(memory_space=pltpu.SMEM), whole, whole],
        [whole, whole],
        [shape, shape],
        flops=near.size,
        vmem=20,
    )(core.reshape(1), near, far)


def shards(
    tokens, cotangent, routes, gates, w_gate_up, w_down, m_gate_up, v_gate_up, m_down, v_down
):
    n_data, n_chip, n_core = (lax.axis_size(a) for a in ("z", "p", "c"))
    pair = n_chip // EXPERTS
    tok_rows, width = tokens.shape
    half = width // n_core
    block = n_core * CAPACITY
    hid = w_down.shape[0]
    c = lax.axis_index("c")
    orders = [
        [((z + k * n_data // n_core) % n_data) * n_core + k for z in range(n_data)]
        for k in range(n_core)
    ]

    flat = routes.reshape(-1)
    place = flat * block + c * CAPACITY + slots_of(flat)
    info = jnp.concatenate([place.astype(jnp.float32)[:, None], gates], axis=1)
    info2 = jnp.concatenate([info, lax.ppermute(info, "c", SWAP)], axis=0)
    place2 = info2[:, 0].astype(jnp.int32)
    gate2 = info2[:, 1:2]
    cot = (gates * cotangent.astype(jnp.float32)).astype(jnp.bfloat16)

    def half_of(array, k):
        return lax.dynamic_slice_in_dim(array, k * half, half, axis=1)

    def both_of(k):
        return jnp.concatenate([half_of(tokens, k), half_of(cot, k)], axis=1)

    sent, w_up, w_dn = lax.optimization_barrier((both_of(1 - c), w_gate_up, w_down))
    owned = jnp.concatenate([w_up[0], w_up[1], w_dn.T], axis=1)
    weights = lax.all_gather(owned, ("z", "c"), axis=0, tiled=True, axis_index_groups=orders)
    rows2 = jnp.concatenate([both_of(c), lax.ppermute(sent, "c", SWAP)], axis=0)
    row_id = lax.broadcasted_iota(jnp.int32, (EXPERTS, pair, block), 0) * block + (
        lax.broadcasted_iota(jnp.int32, (EXPERTS, pair, block), 2)
    )
    row_id = row_id.reshape(-1)
    pick = (row_id[:, None] == place2[None, :]).astype(jnp.bfloat16)
    packed = dot(pick, rows2).astype(jnp.bfloat16).reshape(n_chip, block, width)
    got = lax.all_to_all(packed, "p", split_axis=0, concat_axis=0, tiled=True)
    got, place2, gate2 = lax.optimization_barrier((got, place2, gate2))
    mine = got.reshape(n_chip * block, width)
    unpick = (place2[:, None] == row_id[None, :]).astype(jnp.bfloat16)
    gate2 = jnp.broadcast_to(gate2, (gate2.shape[0], LANES))
    other = lax.ppermute(mine, "c", SWAP)

    weights_o = lax.ppermute(weights[half:], "c", SWAP)
    ready, unpick, gate2 = lax.optimization_barrier((mine, unpick, gate2))
    pre = first_half(ready, weights, hid, BLOCKS)
    deriv, grad = second_half(pre, other, weights, hid, BLOCKS)
    deriv, weights_o = lax.optimization_barrier((deriv, weights_o))
    deriv_o = lax.ppermute(deriv, "c", SWAP)
    grad = first_grads(mine, deriv, grad, hid, BLOCKS)
    grad, deriv_o = lax.optimization_barrier((grad, deriv_o))
    grad = lax.psum_scatter(
        grad, ("z", "c"), scatter_dimension=0, tiled=True, axis_index_groups=orders
    ).astype(jnp.float32)

    back = sent_back(deriv, deriv_o, weights, weights_o, hid, BLOCKS)
    back = lax.all_to_all(
        back.reshape(n_chip, block, width), "p", split_axis=0, concat_axis=0, tiled=True
    ).reshape(n_chip * block, width)
    near, far = unpacked(unpick, gate2, back)
    far = lax.ppermute(far, "c", SWAP)
    scale = (tok_rows * n_data * n_chip * n_core * routes.shape[1] / EXPERTS) ** (-0.5)
    grad_up = jnp.stack([grad[:, :hid], grad[:, hid : 2 * hid]])
    new_wu, new_mu, new_vu = adam_update(w_gate_up, m_gate_up, v_gate_up, grad_up, scale)
    new_wd, new_md, new_vd = adam_update(w_down, m_down, v_down, grad[:, 2 * hid :].T, scale)
    far, new_mu = lax.optimization_barrier((far, new_mu))
    outputs, input_grads = joined(c, near, far)
    return (outputs, input_grads, new_wu, new_mu, new_vu, new_wd, new_md, new_vd)


def solution(mesh):
    n_data, n_expert = (mesh.shape[a] for a in ("dp", "expert"))
    cores = Mesh(mesh.devices.reshape(n_data, n_expert // 2, 2), ("z", "p", "c"))
    rows = P(("z", "p", "c"), None)
    up, down = P(None, "z", ("p", "c")), P(("p", "c"), "z")
    return jax.shard_map(
        shards,
        mesh=cores,
        in_specs=(rows, rows, rows, rows, up, down, up, up, down, down),
        out_specs=(rows, rows, up, up, up, down, down, down),
        check_vma=False,
    )
```

```python
import functools

import jax
import jax.numpy as jnp
from jax import lax
from jax.experimental import pallas as pl
from jax.experimental.pallas import tpu as pltpu
from jax.sharding import Mesh, PartitionSpec as P

EXPERTS = 8
CAPACITY = 20


first_decay = 0.9
second_decay = 0.95
first_correction = 1.0 - 0.9**50 * 0.9**50
second_correction = 1.0 - 0.95**50 * 0.95**50
learn_rate = 0.01
adam_epsilon = 1e-08

SWAP = [(0, 1), (1, 0)]
BLOCKS = 2


def slots_of(flat_routes):
    n = flat_routes.shape[0]
    onehot = (flat_routes[:, None] == jnp.arange(EXPERTS, dtype=jnp.int32)[None, :]).astype(jnp.bfloat16)
    earlier = (jnp.arange(n)[:, None] > jnp.arange(n)[None, :]).astype(jnp.bfloat16)
    before = jnp.dot(earlier, onehot, preferred_element_type=jnp.float32)
    return jnp.sum(before * onehot.astype(jnp.float32), axis=1).astype(jnp.int32)


def adam_update(weight, moment, second, grad_sum, scale):
    grad = grad_sum * scale
    moment_new = first_decay * moment + (1.0 - first_decay) * grad
    second_new = second_decay * second + (1.0 - second_decay) * grad * grad
    update = (
        moment_new / first_correction / (jnp.sqrt(second_new / second_correction) + adam_epsilon)
    )
    weight_new = (weight.astype(jnp.float32) - learn_rate * update).astype(jnp.bfloat16)
    return (weight_new, moment_new, second_new)


def dot(a, b, dims=((1,), (0,))):
    return lax.dot_general(a, b, (dims, ((), ())), preferred_element_type=jnp.float32)


MIB = 1 << 20
VMEM = 56
BACK_VMEM = 50
LANES = 128


def call(body, grid, in_specs, out_specs, out_shape, flops, scratch=(), vmem=VMEM):
    return pl.pallas_call(
        body,
        grid=(grid,),
        in_specs=in_specs,
        out_specs=out_specs,
        out_shape=out_shape,
        scratch_shapes=list(scratch),
        compiler_params=pltpu.CompilerParams(vmem_limit_bytes=vmem * MIB),
        cost_estimate=pl.CostEstimate(flops=flops, bytes_accessed=12 * MIB, transcendentals=0),
    )


def pre_body(hid, x_ref, y_ref, w_ref, acc_ref):
    @pl.when(pl.program_id(0) == 0)
    def _():
        acc_ref[...] = jnp.zeros_like(acc_ref)

    acc_ref[:, : 2 * hid] += dot(x_ref[...], w_ref[:, : 2 * hid])
    acc_ref[:, 2 * hid :] += dot(y_ref[...], w_ref[:, 2 * hid :])


def first_half(rows, weights, hid, blocks):
    n, width = rows.shape
    cols = width // 2 // blocks
    return call(
        functools.partial(pre_body, hid),
        blocks,
        [
            pl.BlockSpec((n, cols), lambda i: (0, i)),
            pl.BlockSpec((n, cols), lambda i: (0, blocks + i)),
            pl.BlockSpec((cols, 3 * hid), lambda i: (i, 0)),
        ],
        pl.BlockSpec((n, 3 * hid), lambda i: (0, 0)),
        jax.ShapeDtypeStruct((n, 3 * hid), jnp.float32),
        flops=3 * n * width * hid,
    )(rows, rows, weights)


def write_grads(hid, x, y, deriv_ref, grad_ref):
    grad_ref[:, : 2 * hid] = dot(x, deriv_ref[:, : 2 * hid], ((0,), (0,))).astype(jnp.bfloat16)
    grad_ref[:, 2 * hid :] = dot(y, deriv_ref[:, 2 * hid :], ((0,), (0,))).astype(jnp.bfloat16)


def mid_body(hid, blocks, pre_ref, xm_ref, ym_ref, xo_ref, yo_ref, w_ref, deriv_ref, grad_ref, acc_ref):
    step = pl.program_id(0)

    @pl.when(step == 0)
    def _():
        acc_ref[...] = pre_ref[...]

    @pl.when(step < blocks)
    def _():
        acc_ref[:, : 2 * hid] += dot(xo_ref[...], w_ref[:, : 2 * hid])
        acc_ref[:, 2 * hid :] += dot(yo_ref[...], w_ref[:, 2 * hid :])

    @pl.when(step == blocks - 1)
    def _():
        act, linear, d_hidden = (acc_ref[:, k * hid : (k + 1) * hid] for k in range(3))
        sig = jax.nn.sigmoid(act)
        gated = act * sig
        deriv_ref[:, :hid] = (d_hidden * linear * sig * (1.0 + act * (1.0 - sig))).astype(jnp.bfloat16)
        deriv_ref[:, hid : 2 * hid] = (d_hidden * gated).astype(jnp.bfloat16)
        deriv_ref[:, 2 * hid :] = (gated * linear).astype(jnp.bfloat16)

    @pl.when((step >= blocks) & (step < 2 * blocks))
    def _():
        write_grads(hid, xo_ref[...], yo_ref[...], deriv_ref, grad_ref)

    @pl.when(step >= 2 * blocks)
    def _():
        write_grads(hid, xm_ref[...], ym_ref[...], deriv_ref, grad_ref)


def second_half(pre, mine, other, weights, hid, blocks):
    n, width = mine.shape
    cols = width // 2 // blocks

    def at(i):
        return jnp.clip(jnp.minimum(i, 2 * blocks - 1 - i), 0, blocks - 1)

    def late(i):
        return jnp.maximum(i - 2 * blocks, 0)

    def grad_at(i):
        return jnp.where(i < blocks, 2 * blocks - 1, jnp.where(i < 2 * blocks, blocks + at(i), late(i)))

    return call(
        functools.partial(mid_body, hid, blocks),
        3 * blocks,
        [
            pl.BlockSpec((n, 3 * hid), lambda i: (0, 0)),
            pl.BlockSpec((n, cols), lambda i: (0, late(i))),
            pl.BlockSpec((n, cols), lambda i: (0, blocks + late(i))),
            pl.BlockSpec((n, cols), lambda i: (0, at(i))),
            pl.BlockSpec((n, cols), lambda i: (0, blocks + at(i))),
            pl.BlockSpec((cols, 3 * hid), lambda i: (blocks + jnp.minimum(i, blocks - 1), 0)),
        ],
        [
            pl.BlockSpec((n, 3 * hid), lambda i: (0, 0)),
            pl.BlockSpec((cols, 3 * hid), lambda i: (grad_at(i), 0)),
        ],
        [
            jax.ShapeDtypeStruct((n, 3 * hid), jnp.bfloat16),
            jax.ShapeDtypeStruct((width, 3 * hid), jnp.bfloat16),
        ],
        flops=9 * n * width * hid,
        scratch=[pltpu.VMEM((n, 3 * hid), jnp.float32)],
    )(pre, mine, mine, other, other, weights)


def back_body(hid, deriv_m_ref, deriv_o_ref, w_m_ref, w_o_ref, back_ref):
    def write(cols):
        mine = dot(deriv_m_ref[:, cols], w_m_ref[:, cols], ((1,), (1,)))
        other = dot(deriv_o_ref[:, cols], w_o_ref[:, cols], ((1,), (1,)))
        back_ref[...] = (mine + other).astype(jnp.bfloat16)

    @pl.when(lax.rem(pl.program_id(0), 2) == 0)
    def _():
        write(slice(2 * hid, 3 * hid))

    @pl.when(lax.rem(pl.program_id(0), 2) == 1)
    def _():
        write(slice(0, 2 * hid))


def sent_back(deriv_m, deriv_o, w_m, w_o, hid, blocks):
    n, width = deriv_m.shape[0], w_m.shape[0]
    cols = width // 2 // blocks
    deriv = pl.BlockSpec((n, 3 * hid), lambda i: (0, 0))
    return call(
        functools.partial(back_body, hid),
        2 * blocks,
        [
            deriv,
            deriv,
            pl.BlockSpec((cols, 3 * hid), lambda i: (lax.div(i, 2), 0)),
            pl.BlockSpec((cols, 3 * hid), lambda i: (blocks + lax.div(i, 2), 0)),
        ],
        pl.BlockSpec((n, cols), lambda i: (0, lax.div(i, 2) + blocks * lax.rem(i, 2))),
        jax.ShapeDtypeStruct((n, width), jnp.bfloat16),
        flops=6 * n * width * hid,
        vmem=BACK_VMEM,
    )(deriv_m, deriv_o, w_m, w_o)


def unpack_body(pick_ref, gate_ref, back_ref, near_ref, far_ref):
    n = near_ref.shape[0]
    picked = dot(pick_ref[...], back_ref[...])
    picked = picked * jnp.where(pl.program_id(0) == 0, gate_ref[:, :1], 1.0)
    near_ref[...] = picked[:n].astype(jnp.bfloat16)
    far_ref[...] = picked[n:].astype(jnp.bfloat16)


def unpacked(pick, gate, back):
    tokens, rows = pick.shape
    half = back.shape[1] // 2
    result = pl.BlockSpec((tokens // 2, half), lambda i: (0, i))
    shape = jax.ShapeDtypeStruct((tokens // 2, 2 * half), jnp.bfloat16)
    return call(
        unpack_body,
        2,
        [
            pl.BlockSpec((tokens, rows), lambda i: (0, 0)),
            pl.BlockSpec((tokens, LANES), lambda i: (0, 0)),
            pl.BlockSpec((rows, half), lambda i: (0, i)),
        ],
        [result, result],
        [shape, shape],
        flops=4 * tokens * rows * half,
        vmem=20,
    )(pick, gate, back)


def join_body(core_ref, near_ref, far_ref, out_ref, grad_ref):
    half = near_ref.shape[1] // 2
    first = core_ref[0] == 0
    for ref, cols in ((out_ref, slice(0, half)), (grad_ref, slice(half, 2 * half))):
        near, far = near_ref[:, cols], far_ref[:, cols]
        ref[:, :half] = jnp.where(first, near, far)
        ref[:, half:] = jnp.where(first, far, near)


def joined(core, near, far):
    whole = pl.BlockSpec(near.shape, lambda i: (0, 0))
    shape = jax.ShapeDtypeStruct(near.shape, jnp.bfloat16)
    return call(
        join_body,
        1,
        [pl.BlockSpec(memory_space=pltpu.SMEM), whole, whole],
        [whole, whole],
        [shape, shape],
        flops=near.size,
        vmem=20,
    )(core.reshape(1), near, far)


def shards(
    tokens, cotangent, routes, gates, w_gate_up, w_down, m_gate_up, v_gate_up, m_down, v_down
):
    n_data, n_chip, n_core = (lax.axis_size(a) for a in ("z", "p", "c"))
    pair = n_chip // EXPERTS
    tok_rows, width = tokens.shape
    half = width // n_core
    block = n_core * CAPACITY
    hid = w_down.shape[0]
    c = lax.axis_index("c")
    orders = [
        [((z + k * n_data // n_core) % n_data) * n_core + k for z in range(n_data)]
        for k in range(n_core)
    ]

    owned = jnp.concatenate([w_gate_up[0], w_gate_up[1], w_down.T], axis=1)
    weights = lax.all_gather(owned, ("z", "c"), axis=0, tiled=True, axis_index_groups=orders)

    flat = routes.reshape(-1)
    place = flat * block + c * CAPACITY + slots_of(flat)
    info = jnp.concatenate([place.astype(jnp.float32)[:, None], gates], axis=1)
    info2 = jnp.concatenate([info, lax.ppermute(info, "c", SWAP)], axis=0)
    place2 = info2[:, 0].astype(jnp.int32)
    gate2 = info2[:, 1:2]
    cot = (gates * cotangent.astype(jnp.float32)).astype(jnp.bfloat16)

    def half_of(array, k):
        return lax.dynamic_slice_in_dim(array, k * half, half, axis=1)

    def both_of(k):
        return jnp.concatenate([half_of(tokens, k), half_of(cot, k)], axis=1)

    rows2 = jnp.concatenate([both_of(c), lax.ppermute(both_of(1 - c), "c", SWAP)], axis=0)
    row_id = lax.broadcasted_iota(jnp.int32, (EXPERTS, pair, block), 0) * block + (
        lax.broadcasted_iota(jnp.int32, (EXPERTS, pair, block), 2)
    )
    row_id = row_id.reshape(-1)
    pick = (row_id[:, None] == place2[None, :]).astype(jnp.bfloat16)
    packed = dot(pick, rows2).astype(jnp.bfloat16).reshape(n_chip, block, width)
    got = lax.all_to_all(packed, "p", split_axis=0, concat_axis=0, tiled=True)
    got, place2, gate2 = lax.optimization_barrier((got, place2, gate2))
    mine = got.reshape(n_chip * block, width)
    unpick = (place2[:, None] == row_id[None, :]).astype(jnp.bfloat16)
    gate2 = jnp.broadcast_to(gate2, (gate2.shape[0], LANES))
    other = lax.ppermute(mine, "c", SWAP)

    ready, unpick, gate2 = lax.optimization_barrier((mine, unpick, gate2))
    pre = first_half(ready, weights, hid, BLOCKS)
    pre, sent = lax.optimization_barrier((pre, weights))
    weights_o = lax.ppermute(sent, "c", SWAP)
    deriv, grad = second_half(pre, mine, other, weights, hid, BLOCKS)
    deriv, weights_o = lax.optimization_barrier((deriv, weights_o))
    deriv_o = lax.ppermute(deriv, "c", SWAP)
    grad = lax.psum_scatter(
        grad, ("z", "c"), scatter_dimension=0, tiled=True, axis_index_groups=orders
    ).astype(jnp.float32)

    back = sent_back(deriv, deriv_o, weights, weights_o, hid, BLOCKS)
    back = lax.all_to_all(
        back.reshape(n_chip, block, width), "p", split_axis=0, concat_axis=0, tiled=True
    ).reshape(n_chip * block, width)
    near, far = unpacked(unpick, gate2, back)
    far = lax.ppermute(far, "c", SWAP)
    scale = (tok_rows * n_data * n_chip * n_core * routes.shape[1] / EXPERTS) ** (-0.5)
    grad_up = jnp.stack([grad[:, :hid], grad[:, hid : 2 * hid]])
    new_wu, new_mu, new_vu = adam_update(w_gate_up, m_gate_up, v_gate_up, grad_up, scale)
    new_wd, new_md, new_vd = adam_update(w_down, m_down, v_down, grad[:, 2 * hid :].T, scale)
    far, new_mu = lax.optimization_barrier((far, new_mu))
    outputs, input_grads = joined(c, near, far)
    return (outputs, input_grads, new_wu, new_mu, new_vu, new_wd, new_md, new_vd)


def solution(mesh):
    n_data, n_expert = (mesh.shape[a] for a in ("dp", "expert"))
    cores = Mesh(mesh.devices.reshape(n_data, n_expert // 2, 2), ("z", "p", "c"))
    rows = P(("z", "p", "c"), None)
    up, down = P(None, "z", ("p", "c")), P(("p", "c"), "z")
    return jax.shard_map(
        shards,
        mesh=cores,
        in_specs=(rows, rows, rows, rows, up, down, up, up, down, down),
        out_specs=(rows, rows, up, up, up, down, down, down),
        check_vma=False,
    )
```

```python
import functools

import jax
import jax.numpy as jnp
from jax import lax
from jax.experimental import pallas as pl
from jax.experimental.pallas import tpu as pltpu
from jax.sharding import Mesh, PartitionSpec as P

EXPERTS = 8
CAPACITY = 20


first_decay = 0.9
second_decay = 0.95
first_correction = 1.0 - 0.9**50 * 0.9**50
second_correction = 1.0 - 0.95**50 * 0.95**50
learn_rate = 0.01
adam_epsilon = 1e-08

SWAP = [(0, 1), (1, 0)]
BLOCKS = 2


def slots_of(flat_routes):
    n = flat_routes.shape[0]
    onehot = (flat_routes[:, None] == jnp.arange(EXPERTS, dtype=jnp.int32)[None, :]).astype(jnp.bfloat16)
    earlier = (jnp.arange(n)[:, None] > jnp.arange(n)[None, :]).astype(jnp.bfloat16)
    before = jnp.dot(earlier, onehot, preferred_element_type=jnp.float32)
    return jnp.sum(before * onehot.astype(jnp.float32), axis=1).astype(jnp.int32)


def adam_update(weight, moment, second, grad_sum, scale):
    grad = grad_sum * scale
    moment_new = first_decay * moment + (1.0 - first_decay) * grad
    second_new = second_decay * second + (1.0 - second_decay) * grad * grad
    update = (
        moment_new / first_correction / (jnp.sqrt(second_new / second_correction) + adam_epsilon)
    )
    weight_new = (weight.astype(jnp.float32) - learn_rate * update).astype(jnp.bfloat16)
    return (weight_new, moment_new, second_new)


def dot(a, b, dims=((1,), (0,))):
    return lax.dot_general(a, b, (dims, ((), ())), preferred_element_type=jnp.float32)


MIB = 1 << 20
FIRST_VMEM = 56
VMEM = 56
BACK_VMEM = 50
LANES = 128


def call(body, grid, in_specs, out_specs, out_shape, flops, scratch=(), vmem=VMEM, size=12 * MIB):
    return pl.pallas_call(
        body,
        grid=(grid,),
        in_specs=in_specs,
        out_specs=out_specs,
        out_shape=out_shape,
        scratch_shapes=list(scratch),
        compiler_params=pltpu.CompilerParams(vmem_limit_bytes=vmem * MIB),
        cost_estimate=pl.CostEstimate(flops=flops, bytes_accessed=size, transcendentals=0),
    )


def lay_body(up_ref, down_ref, out_ref):
    hid = down_ref.shape[1]
    out_ref[:, :hid] = up_ref[0]
    out_ref[:, hid : 2 * hid] = up_ref[1]
    out_ref[:, 2 * hid :] = down_ref[...]


def laid(up, down):
    rows, hid = down.shape
    return call(
        lay_body,
        1,
        [
            pl.BlockSpec((2, rows, hid), lambda i: (0, 0, 0)),
            pl.BlockSpec((rows, hid), lambda i: (0, 0)),
        ],
        pl.BlockSpec((rows, 3 * hid), lambda i: (0, 0)),
        jax.ShapeDtypeStruct((rows, 3 * hid), up.dtype),
        flops=up.size,
        vmem=8,
    )(up, down)


def pre_body(hid, x_ref, y_ref, w_ref, acc_ref):
    @pl.when(pl.program_id(0) == 0)
    def _():
        acc_ref[...] = jnp.zeros_like(acc_ref)

    acc_ref[:, : 2 * hid] += dot(x_ref[...], w_ref[:, : 2 * hid])
    acc_ref[:, 2 * hid :] += dot(y_ref[...], w_ref[:, 2 * hid :])


def first_half(rows, weights, hid, blocks):
    n, width = rows.shape
    cols = width // 2 // blocks
    return call(
        functools.partial(pre_body, hid),
        blocks,
        [
            pl.BlockSpec((n, cols), lambda i: (0, i)),
            pl.BlockSpec((n, cols), lambda i: (0, blocks + i)),
            pl.BlockSpec((cols, 3 * hid), lambda i: (i, 0)),
        ],
        pl.BlockSpec((n, 3 * hid), lambda i: (0, 0)),
        jax.ShapeDtypeStruct((n, 3 * hid), jnp.float32),
        flops=n * hid,
        vmem=FIRST_VMEM,
        size=MIB >> 4,
    )(rows, rows, weights)


def write_grads(hid, x, y, deriv_ref, grad_ref):
    grad_ref[:, : 2 * hid] = dot(x, deriv_ref[:, : 2 * hid], ((0,), (0,))).astype(jnp.bfloat16)
    grad_ref[:, 2 * hid :] = dot(y, deriv_ref[:, 2 * hid :], ((0,), (0,))).astype(jnp.bfloat16)


def mid_body(hid, blocks, pre_ref, x_ref, y_ref, w_ref, deriv_ref, grad_ref, acc_ref):
    step = pl.program_id(0)

    @pl.when(step == 0)
    def _():
        acc_ref[...] = pre_ref[...]

    @pl.when(step < blocks)
    def _():
        acc_ref[:, : 2 * hid] += dot(x_ref[...], w_ref[:, : 2 * hid])
        acc_ref[:, 2 * hid :] += dot(y_ref[...], w_ref[:, 2 * hid :])

    @pl.when(step == blocks - 1)
    def _():
        act, linear, d_hidden = (acc_ref[:, k * hid : (k + 1) * hid] for k in range(3))
        sig = jax.nn.sigmoid(act)
        gated = act * sig
        deriv_ref[:, :hid] = (d_hidden * linear * sig * (1.0 + act * (1.0 - sig))).astype(jnp.bfloat16)
        deriv_ref[:, hid : 2 * hid] = (d_hidden * gated).astype(jnp.bfloat16)
        deriv_ref[:, 2 * hid :] = (gated * linear).astype(jnp.bfloat16)

    @pl.when(step >= blocks)
    def _():
        write_grads(hid, x_ref[...], y_ref[...], deriv_ref, grad_ref)


def second_half(pre, rows, weights, hid, blocks):
    n, width = rows.shape
    cols = width // 2 // blocks

    def at(i):
        return jnp.minimum(i, 2 * blocks - 1 - i)

    return call(
        functools.partial(mid_body, hid, blocks),
        2 * blocks,
        [
            pl.BlockSpec((n, 3 * hid), lambda i: (0, 0)),
            pl.BlockSpec((n, cols), lambda i: (0, at(i))),
            pl.BlockSpec((n, cols), lambda i: (0, blocks + at(i))),
            pl.BlockSpec((cols, 3 * hid), lambda i: (blocks + jnp.minimum(i, blocks - 1), 0)),
        ],
        [
            pl.BlockSpec((n, 3 * hid), lambda i: (0, 0)),
            pl.BlockSpec((cols, 3 * hid), lambda i: (blocks + jnp.minimum(blocks - 1, 2 * blocks - 1 - i), 0)),
        ],
        [
            jax.ShapeDtypeStruct((n, 3 * hid), jnp.bfloat16),
            jax.ShapeDtypeStruct((width, 3 * hid), jnp.bfloat16),
        ],
        flops=6 * n * width * hid,
        scratch=[pltpu.VMEM((n, 3 * hid), jnp.float32)],
    )(pre, rows, rows, weights)


def grad_body(hid, x_ref, y_ref, deriv_ref, _, grad_ref):
    write_grads(hid, x_ref[...], y_ref[...], deriv_ref, grad_ref)


def first_grads(rows, deriv, grad, hid, blocks):
    n, width = rows.shape
    cols = width // 2 // blocks
    return pl.pallas_call(
        functools.partial(grad_body, hid),
        grid=(blocks,),
        in_specs=[
            pl.BlockSpec((n, cols), lambda i: (0, i)),
            pl.BlockSpec((n, cols), lambda i: (0, blocks + i)),
            pl.BlockSpec((n, 3 * hid), lambda i: (0, 0)),
            pl.BlockSpec(memory_space=pl.ANY),
        ],
        out_specs=pl.BlockSpec((cols, 3 * hid), lambda i: (i, 0)),
        out_shape=jax.ShapeDtypeStruct((width, 3 * hid), jnp.bfloat16),
        input_output_aliases={3: 0},
        compiler_params=pltpu.CompilerParams(vmem_limit_bytes=VMEM * MIB),
        cost_estimate=pl.CostEstimate(flops=3 * n * width * hid, bytes_accessed=12 * MIB, transcendentals=0),
    )(rows, rows, deriv, grad)


def back_body(hid, deriv_m_ref, deriv_o_ref, w_m_ref, w_o_ref, back_ref):
    def write(cols):
        mine = dot(deriv_m_ref[:, cols], w_m_ref[:, cols], ((1,), (1,)))
        other = dot(deriv_o_ref[:, cols], w_o_ref[:, cols], ((1,), (1,)))
        back_ref[...] = (mine + other).astype(jnp.bfloat16)

    @pl.when(lax.rem(pl.program_id(0), 2) == 0)
    def _():
        write(slice(2 * hid, 3 * hid))

    @pl.when(lax.rem(pl.program_id(0), 2) == 1)
    def _():
        write(slice(0, 2 * hid))


def sent_back(deriv_m, deriv_o, w_m, w_o, hid, blocks):
    n, width = deriv_m.shape[0], w_m.shape[0]
    cols = width // 2 // blocks
    deriv = pl.BlockSpec((n, 3 * hid), lambda i: (0, 0))
    return call(
        functools.partial(back_body, hid),
        2 * blocks,
        [
            deriv,
            deriv,
            pl.BlockSpec((cols, 3 * hid), lambda i: (lax.div(i, 2), 0)),
            pl.BlockSpec((cols, 3 * hid), lambda i: (blocks + lax.div(i, 2), 0)),
        ],
        pl.BlockSpec((n, cols), lambda i: (0, lax.div(i, 2) + blocks * lax.rem(i, 2))),
        jax.ShapeDtypeStruct((n, width), jnp.bfloat16),
        flops=6 * n * width * hid,
        vmem=BACK_VMEM,
    )(deriv_m, deriv_o, w_m, w_o)


def unpack_body(pick_ref, gate_ref, back_ref, near_ref, far_ref):
    n = near_ref.shape[0]
    picked = dot(pick_ref[...], back_ref[...])
    picked = picked * jnp.where(pl.program_id(0) == 0, gate_ref[:, :1], 1.0)
    near_ref[...] = picked[:n].astype(jnp.bfloat16)
    far_ref[...] = picked[n:].astype(jnp.bfloat16)


def unpacked(pick, gate, back):
    tokens, rows = pick.shape
    half = back.shape[1] // 2
    result = pl.BlockSpec((tokens // 2, half), lambda i: (0, i))
    shape = jax.ShapeDtypeStruct((tokens // 2, 2 * half), jnp.bfloat16)
    return call(
        unpack_body,
        2,
        [
            pl.BlockSpec((tokens, rows), lambda i: (0, 0)),
            pl.BlockSpec((tokens, LANES), lambda i: (0, 0)),
            pl.BlockSpec((rows, half), lambda i: (0, i)),
        ],
        [result, result],
        [shape, shape],
        flops=4 * tokens * rows * half,
        vmem=20,
    )(pick, gate, back)


def join_body(core_ref, near_ref, far_ref, out_ref, grad_ref):
    half = near_ref.shape[1] // 2
    first = core_ref[0] == 0
    for ref, cols in ((out_ref, slice(0, half)), (grad_ref, slice(half, 2 * half))):
        near, far = near_ref[:, cols], far_ref[:, cols]
        ref[:, :half] = jnp.where(first, near, far)
        ref[:, half:] = jnp.where(first, far, near)


def joined(core, near, far):
    whole = pl.BlockSpec(near.shape, lambda i: (0, 0))
    shape = jax.ShapeDtypeStruct(near.shape, jnp.bfloat16)
    return call(
        join_body,
        1,
        [pl.BlockSpec(memory_space=pltpu.SMEM), whole, whole],
        [whole, whole],
        [shape, shape],
        flops=near.size,
        vmem=20,
    )(core.reshape(1), near, far)


def shards(
    tokens, cotangent, routes, gates, w_gate_up, w_down, m_gate_up, v_gate_up, m_down, v_down
):
    n_data, n_chip, n_core = (lax.axis_size(a) for a in ("z", "p", "c"))
    pair = n_chip // EXPERTS
    tok_rows, width = tokens.shape
    half = width // n_core
    block = n_core * CAPACITY
    hid = w_down.shape[0]
    c = lax.axis_index("c")
    orders = [
        [((z + k * n_data // n_core) % n_data) * n_core + k for z in range(n_data)]
        for k in range(n_core)
    ]

    owned = laid(w_gate_up, w_down.T)
    weights = lax.all_gather(owned, ("z", "c"), axis=0, tiled=True, axis_index_groups=orders)

    cot = (gates * cotangent.astype(jnp.float32)).astype(jnp.bfloat16)

    def half_of(array, k):
        return lax.dynamic_slice_in_dim(array, k * half, half, axis=1)

    def both_of(k):
        return jnp.concatenate([half_of(tokens, k), half_of(cot, k)], axis=1)

    sent, routes, gates = lax.optimization_barrier((both_of(1 - c), routes, gates))
    rows2 = jnp.concatenate([both_of(c), lax.ppermute(sent, "c", SWAP)], axis=0)
    flat = routes.reshape(-1)
    place = flat * block + c * CAPACITY + slots_of(flat)
    info = jnp.concatenate([place.astype(jnp.float32)[:, None], gates], axis=1)
    info2 = jnp.concatenate([info, lax.ppermute(info, "c", SWAP)], axis=0)
    place2 = info2[:, 0].astype(jnp.int32)
    gate2 = info2[:, 1:2]
    row_id = lax.broadcasted_iota(jnp.int32, (EXPERTS, pair, block), 0) * block + (
        lax.broadcasted_iota(jnp.int32, (EXPERTS, pair, block), 2)
    )
    row_id = row_id.reshape(-1)
    pick = (row_id[:, None] == place2[None, :]).astype(jnp.bfloat16)
    packed = dot(pick, rows2).astype(jnp.bfloat16).reshape(n_chip, block, width)
    got = lax.all_to_all(packed, "p", split_axis=0, concat_axis=0, tiled=True)
    got, place2, gate2 = lax.optimization_barrier((got, place2, gate2))
    mine = got.reshape(n_chip * block, width)
    unpick = (place2[:, None] == row_id[None, :]).astype(jnp.bfloat16)
    gate2 = jnp.broadcast_to(gate2, (gate2.shape[0], LANES))
    other = lax.ppermute(mine, "c", SWAP)

    ready, unpick, gate2 = lax.optimization_barrier((mine, unpick, gate2))
    pre = first_half(ready, weights, hid, BLOCKS)
    pre, other, sent = lax.optimization_barrier((pre, other, weights))
    weights_o = lax.ppermute(sent, "c", SWAP)
    deriv, grad = second_half(pre, other, weights, hid, BLOCKS)
    deriv, weights_o = lax.optimization_barrier((deriv, weights_o))
    deriv_o = lax.ppermute(deriv, "c", SWAP)
    grad = first_grads(mine, deriv, grad, hid, BLOCKS)
    grad, deriv_o = lax.optimization_barrier((grad, deriv_o))
    grad = lax.psum_scatter(
        grad, ("z", "c"), scatter_dimension=0, tiled=True, axis_index_groups=orders
    ).astype(jnp.float32)

    back = sent_back(deriv, deriv_o, weights, weights_o, hid, BLOCKS)
    back = lax.all_to_all(
        back.reshape(n_chip, block, width), "p", split_axis=0, concat_axis=0, tiled=True
    ).reshape(n_chip * block, width)
    near, far = unpacked(unpick, gate2, back)
    far = lax.ppermute(far, "c", SWAP)
    scale = (tok_rows * n_data * n_chip * n_core * routes.shape[1] / EXPERTS) ** (-0.5)
    grad_up = jnp.stack([grad[:, :hid], grad[:, hid : 2 * hid]])
    new_wu, new_mu, new_vu = adam_update(w_gate_up, m_gate_up, v_gate_up, grad_up, scale)
    new_wd, new_md, new_vd = adam_update(w_down, m_down, v_down, grad[:, 2 * hid :].T, scale)
    far, new_mu = lax.optimization_barrier((far, new_mu))
    outputs, input_grads = joined(c, near, far)
    return (outputs, input_grads, new_wu, new_mu, new_vu, new_wd, new_md, new_vd)


def solution(mesh):
    n_data, n_expert = (mesh.shape[a] for a in ("dp", "expert"))
    cores = Mesh(mesh.devices.reshape(n_data, n_expert // 2, 2), ("z", "p", "c"))
    rows = P(("z", "p", "c"), None)
    up, down = P(None, "z", ("p", "c")), P(("p", "c"), "z")
    return jax.shard_map(
        shards,
        mesh=cores,
        in_specs=(rows, rows, rows, rows, up, down, up, up, down, down),
        out_specs=(rows, rows, up, up, up, down, down, down),
        check_vma=False,
    )
```

```python
import functools

import jax
import jax.numpy as jnp
from jax import lax
from jax.experimental import pallas as pl
from jax.experimental.pallas import tpu as pltpu
from jax.sharding import Mesh, PartitionSpec as P

EXPERTS = 8
CAPACITY = 20


first_decay = 0.9
second_decay = 0.95
first_correction = 1.0 - 0.9**50 * 0.9**50
second_correction = 1.0 - 0.95**50 * 0.95**50
learn_rate = 0.01
adam_epsilon = 1e-08

SWAP = [(0, 1), (1, 0)]
BLOCKS = 2


def slots_of(flat_routes):
    n = flat_routes.shape[0]
    onehot = (flat_routes[:, None] == jnp.arange(EXPERTS, dtype=jnp.int32)[None, :]).astype(jnp.bfloat16)
    earlier = (jnp.arange(n)[:, None] > jnp.arange(n)[None, :]).astype(jnp.bfloat16)
    before = jnp.dot(earlier, onehot, preferred_element_type=jnp.float32)
    return jnp.sum(before * onehot.astype(jnp.float32), axis=1).astype(jnp.int32)


def adam_update(weight, moment, second, grad_sum, scale):
    grad = grad_sum * scale
    moment_new = first_decay * moment + (1.0 - first_decay) * grad
    second_new = second_decay * second + (1.0 - second_decay) * grad * grad
    update = (
        moment_new / first_correction / (jnp.sqrt(second_new / second_correction) + adam_epsilon)
    )
    weight_new = (weight.astype(jnp.float32) - learn_rate * update).astype(jnp.bfloat16)
    return (weight_new, moment_new, second_new)


def dot(a, b, dims=((1,), (0,))):
    return lax.dot_general(a, b, (dims, ((), ())), preferred_element_type=jnp.float32)


MIB = 1 << 20
UPDATE_BLOCKS = 4
FIRST_VMEM = 56
VMEM = 56
BACK_VMEM = 28
LANES = 128


def in_hbm(array):
    return pltpu.with_memory_space_constraint(array, pltpu.HBM)


def in_vmem(array):
    return pltpu.with_memory_space_constraint(array, pltpu.VMEM)


def call(body, grid, in_specs, out_specs, out_shape, flops, scratch=(), vmem=VMEM, size=12 * MIB):
    return pl.pallas_call(
        body,
        grid=(grid,),
        in_specs=in_specs,
        out_specs=out_specs,
        out_shape=out_shape,
        scratch_shapes=list(scratch),
        compiler_params=pltpu.CompilerParams(vmem_limit_bytes=vmem * MIB),
        cost_estimate=pl.CostEstimate(flops=flops, bytes_accessed=size, transcendentals=0),
    )


def lay_body(up_ref, down_ref, out_ref):
    hid = down_ref.shape[1]
    out_ref[:, :hid] = up_ref[0]
    out_ref[:, hid : 2 * hid] = up_ref[1]
    out_ref[:, 2 * hid :] = down_ref[...]


def laid(up, down):
    rows, hid = down.shape
    return call(
        lay_body,
        1,
        [
            pl.BlockSpec((2, rows, hid), lambda i: (0, 0, 0)),
            pl.BlockSpec((rows, hid), lambda i: (0, 0)),
        ],
        pl.BlockSpec((rows, 3 * hid), lambda i: (0, 0)),
        jax.ShapeDtypeStruct((rows, 3 * hid), up.dtype),
        flops=up.size,
        vmem=56,
    )(up, down)


def pre_body(hid, x_ref, y_ref, w_ref, acc_ref):
    @pl.when(pl.program_id(0) == 0)
    def _():
        acc_ref[...] = jnp.zeros_like(acc_ref)

    acc_ref[:, : 2 * hid] += dot(x_ref[...], w_ref[:, : 2 * hid])
    acc_ref[:, 2 * hid :] += dot(y_ref[...], w_ref[:, 2 * hid :])


def first_half(rows, weights, hid, blocks):
    n, width = rows.shape
    cols = width // 2 // blocks
    return call(
        functools.partial(pre_body, hid),
        blocks,
        [
            pl.BlockSpec((n, cols), lambda i: (0, i)),
            pl.BlockSpec((n, cols), lambda i: (0, blocks + i)),
            pl.BlockSpec((cols, 3 * hid), lambda i: (i, 0)),
        ],
        pl.BlockSpec((n, 3 * hid), lambda i: (0, 0)),
        pltpu.VMEM((n, 3 * hid), jnp.float32),
        flops=n * hid,
        vmem=FIRST_VMEM,
        size=MIB >> 4,
    )(in_hbm(rows), in_hbm(rows), in_hbm(weights))


def write_grads(hid, x, y, deriv_ref, grad_ref):
    grad_ref[:, : 2 * hid] = dot(x, deriv_ref[:, : 2 * hid], ((0,), (0,))).astype(jnp.bfloat16)
    grad_ref[:, 2 * hid :] = dot(y, deriv_ref[:, 2 * hid :], ((0,), (0,))).astype(jnp.bfloat16)


def mid_body(hid, blocks, pre_ref, x_ref, y_ref, w_ref, deriv_ref, grad_ref, acc_ref):
    step = pl.program_id(0)

    @pl.when(step == 0)
    def _():
        acc_ref[...] = pre_ref[...]

    @pl.when(step < blocks)
    def _():
        acc_ref[:, : 2 * hid] += dot(x_ref[...], w_ref[:, : 2 * hid])
        acc_ref[:, 2 * hid :] += dot(y_ref[...], w_ref[:, 2 * hid :])

    @pl.when(step == blocks - 1)
    def _():
        act, linear, d_hidden = (acc_ref[:, k * hid : (k + 1) * hid] for k in range(3))
        sig = jax.nn.sigmoid(act)
        gated = act * sig
        deriv_ref[:, :hid] = (d_hidden * linear * sig * (1.0 + act * (1.0 - sig))).astype(jnp.bfloat16)
        deriv_ref[:, hid : 2 * hid] = (d_hidden * gated).astype(jnp.bfloat16)
        deriv_ref[:, 2 * hid :] = (gated * linear).astype(jnp.bfloat16)

    @pl.when(step >= blocks)
    def _():
        write_grads(hid, x_ref[...], y_ref[...], deriv_ref, grad_ref)


def second_half(pre, rows, weights, hid, blocks):
    n, width = rows.shape
    cols = width // 2 // blocks

    def at(i):
        return jnp.minimum(i, 2 * blocks - 1 - i)

    return call(
        functools.partial(mid_body, hid, blocks),
        2 * blocks,
        [
            pl.BlockSpec((n, 3 * hid), lambda i: (0, 0)),
            pl.BlockSpec((n, cols), lambda i: (0, at(i))),
            pl.BlockSpec((n, cols), lambda i: (0, blocks + at(i))),
            pl.BlockSpec((cols, 3 * hid), lambda i: (blocks + jnp.minimum(i, blocks - 1), 0)),
        ],
        [
            pl.BlockSpec((n, 3 * hid), lambda i: (0, 0)),
            pl.BlockSpec((cols, 3 * hid), lambda i: (blocks + jnp.minimum(blocks - 1, 2 * blocks - 1 - i), 0)),
        ],
        [
            pltpu.VMEM((n, 3 * hid), jnp.bfloat16),
            pltpu.HBM((width, 3 * hid), jnp.bfloat16),
        ],
        flops=6 * n * width * hid,
        scratch=[pltpu.VMEM((n, 3 * hid), jnp.float32)],
    )(in_vmem(pre), in_hbm(rows), in_hbm(rows), in_hbm(weights))


def grad_body(hid, x_ref, y_ref, deriv_ref, _, grad_ref):
    write_grads(hid, x_ref[...], y_ref[...], deriv_ref, grad_ref)


def first_grads(rows, deriv, grad, hid, blocks):
    n, width = rows.shape
    cols = width // 2 // blocks
    return pl.pallas_call(
        functools.partial(grad_body, hid),
        grid=(blocks,),
        in_specs=[
            pl.BlockSpec((n, cols), lambda i: (0, i)),
            pl.BlockSpec((n, cols), lambda i: (0, blocks + i)),
            pl.BlockSpec((n, 3 * hid), lambda i: (0, 0)),
            pl.BlockSpec(memory_space=pl.ANY),
        ],
        out_specs=pl.BlockSpec((cols, 3 * hid), lambda i: (i, 0)),
        out_shape=pltpu.HBM((width, 3 * hid), jnp.bfloat16),
        input_output_aliases={3: 0},
        compiler_params=pltpu.CompilerParams(vmem_limit_bytes=VMEM * MIB),
        cost_estimate=pl.CostEstimate(flops=3 * n * width * hid, bytes_accessed=12 * MIB, transcendentals=0),
    )(in_hbm(rows), in_hbm(rows), in_vmem(deriv), in_hbm(grad))


def back_body(hid, deriv_m_ref, deriv_o_ref, w_m_ref, w_o_ref, back_ref):
    def write(cols):
        mine = dot(deriv_m_ref[:, cols], w_m_ref[:, cols], ((1,), (1,)))
        other = dot(deriv_o_ref[:, cols], w_o_ref[:, cols], ((1,), (1,)))
        back_ref[...] = (mine + other).astype(jnp.bfloat16)

    @pl.when(lax.rem(pl.program_id(0), 2) == 0)
    def _():
        write(slice(2 * hid, 3 * hid))

    @pl.when(lax.rem(pl.program_id(0), 2) == 1)
    def _():
        write(slice(0, 2 * hid))


def sent_back(deriv_m, deriv_o, w_m, w_o, hid, blocks):
    n, width = deriv_m.shape[0], w_m.shape[0]
    cols = width // 2 // blocks
    deriv = pl.BlockSpec((n, 3 * hid), lambda i: (0, 0))
    return call(
        functools.partial(back_body, hid),
        2 * blocks,
        [
            deriv,
            deriv,
            pl.BlockSpec((cols, 3 * hid), lambda i: (lax.div(i, 2), 0)),
            pl.BlockSpec((cols, 3 * hid), lambda i: (blocks + lax.div(i, 2), 0)),
        ],
        pl.BlockSpec((n, cols), lambda i: (0, lax.div(i, 2) + blocks * lax.rem(i, 2))),
        pltpu.VMEM((n, width), jnp.bfloat16),
        flops=6 * n * width * hid,
        vmem=BACK_VMEM,
    )(in_vmem(deriv_m), in_vmem(deriv_o), in_hbm(w_m), in_hbm(w_o))


def unpack_body(pick_ref, gate_ref, back_ref, near_ref, far_ref):
    n = near_ref.shape[0]
    picked = dot(pick_ref[...], back_ref[...])
    picked = picked * jnp.where(pl.program_id(0) == 0, gate_ref[:, :1], 1.0)
    near_ref[...] = picked[:n].astype(jnp.bfloat16)
    far_ref[...] = picked[n:].astype(jnp.bfloat16)


def unpacked(pick, gate, back):
    tokens, rows = pick.shape
    half = back.shape[1] // 2
    result = pl.BlockSpec((tokens // 2, half), lambda i: (0, i))
    shape = jax.ShapeDtypeStruct((tokens // 2, 2 * half), jnp.bfloat16)
    return call(
        unpack_body,
        2,
        [
            pl.BlockSpec((tokens, rows), lambda i: (0, 0)),
            pl.BlockSpec((tokens, LANES), lambda i: (0, 0)),
            pl.BlockSpec((rows, half), lambda i: (0, i)),
        ],
        [result, result],
        [shape, shape],
        flops=4 * tokens * rows * half,
        vmem=20,
    )(pick, gate, back)


def update_body(scale, grad_ref, wu_ref, mu_ref, vu_ref, wd_ref, md_ref, vd_ref, *out_refs):
    hid = wd_ref.shape[1]
    for k, (w_ref, m_ref, v_ref) in enumerate(((wu_ref, mu_ref, vu_ref),) * 2 + ((wd_ref, md_ref, vd_ref),)):
        at = (k,) if k < 2 else ()
        grad = grad_ref[:, k * hid : (k + 1) * hid].astype(jnp.float32)
        new = adam_update(w_ref[at + (...,)], m_ref[at + (...,)], v_ref[at + (...,)], grad, scale)
        for ref, value in zip(out_refs[:3] if k < 2 else out_refs[3:], new):
            ref[at + (...,)] = value


def updated(grad, up, down, scale, blocks):
    rows, hid = down[0].shape
    step = rows // blocks
    up_spec = pl.BlockSpec((2, step, hid), lambda i: (0, i, 0))
    down_spec = pl.BlockSpec((step, hid), lambda i: (i, 0))
    return call(
        functools.partial(update_body, scale),
        blocks,
        [pl.BlockSpec((step, 3 * hid), lambda i: (i, 0))] + [up_spec] * 3 + [down_spec] * 3,
        [up_spec] * 3 + [down_spec] * 3,
        [jax.ShapeDtypeStruct(a.shape, a.dtype) for a in (*up, *down)],
        flops=60 * rows * hid,
        vmem=56,
    )(grad, *up, *down)


def join_body(core_ref, near_ref, far_ref, out_ref, grad_ref):
    half = near_ref.shape[1] // 2
    first = core_ref[0] == 0
    for ref, cols in ((out_ref, slice(0, half)), (grad_ref, slice(half, 2 * half))):
        near, far = near_ref[:, cols], far_ref[:, cols]
        ref[:, :half] = jnp.where(first, near, far)
        ref[:, half:] = jnp.where(first, far, near)


def joined(core, near, far):
    whole = pl.BlockSpec(near.shape, lambda i: (0, 0))
    shape = jax.ShapeDtypeStruct(near.shape, jnp.bfloat16)
    return call(
        join_body,
        1,
        [pl.BlockSpec(memory_space=pltpu.SMEM), whole, whole],
        [whole, whole],
        [shape, shape],
        flops=near.size,
        vmem=20,
    )(core.reshape(1), near, far)


def shards(
    tokens, cotangent, routes, gates, w_gate_up, w_down, m_gate_up, v_gate_up, m_down, v_down
):
    n_data, n_chip, n_core = (lax.axis_size(a) for a in ("z", "p", "c"))
    pair = n_chip // EXPERTS
    tok_rows, width = tokens.shape
    half = width // n_core
    block = n_core * CAPACITY
    hid = w_down.shape[0]
    c = lax.axis_index("c")
    orders = [
        [((z + k * n_data // n_core) % n_data) * n_core + k for z in range(n_data)]
        for k in range(n_core)
    ]

    owned = laid(w_gate_up, w_down.T)
    weights = lax.all_gather(owned, ("z", "c"), axis=0, tiled=True, axis_index_groups=orders)

    cot = (gates * cotangent.astype(jnp.float32)).astype(jnp.bfloat16)

    def half_of(array, k):
        return lax.dynamic_slice_in_dim(array, k * half, half, axis=1)

    def both_of(k):
        return jnp.concatenate([half_of(tokens, k), half_of(cot, k)], axis=1)

    sent, routes, gates = lax.optimization_barrier((both_of(1 - c), routes, gates))
    rows2 = jnp.concatenate([both_of(c), lax.ppermute(sent, "c", SWAP)], axis=0)
    flat = routes.reshape(-1)
    place = flat * block + c * CAPACITY + slots_of(flat)
    info = jnp.concatenate([place.astype(jnp.float32)[:, None], gates], axis=1)
    info2 = jnp.concatenate([info, lax.ppermute(info, "c", SWAP)], axis=0)
    place2 = info2[:, 0].astype(jnp.int32)
    gate2 = info2[:, 1:2]
    row_id = lax.broadcasted_iota(jnp.int32, (EXPERTS, pair, block), 0) * block + (
        lax.broadcasted_iota(jnp.int32, (EXPERTS, pair, block), 2)
    )
    row_id = row_id.reshape(-1)
    pick = (row_id[:, None] == place2[None, :]).astype(jnp.bfloat16)
    packed = dot(pick, rows2).astype(jnp.bfloat16).reshape(n_chip, block, width)
    got = lax.all_to_all(packed, "p", split_axis=0, concat_axis=0, tiled=True)
    got, place2, gate2 = lax.optimization_barrier((got, place2, gate2))
    mine = got.reshape(n_chip * block, width)
    unpick = (place2[:, None] == row_id[None, :]).astype(jnp.bfloat16)
    gate2 = jnp.broadcast_to(gate2, (gate2.shape[0], LANES))
    other = lax.ppermute(mine, "c", SWAP)

    ready, unpick, gate2 = lax.optimization_barrier((mine, unpick, gate2))
    pre = first_half(ready, weights, hid, BLOCKS)
    pre, other, sent = lax.optimization_barrier((pre, other, weights))
    weights_o = lax.ppermute(sent, "c", SWAP)
    deriv, grad = second_half(pre, other, weights, hid, BLOCKS)
    deriv, weights_o = lax.optimization_barrier((deriv, weights_o))
    deriv_o = lax.ppermute(deriv, "c", SWAP)
    grad = first_grads(mine, deriv, grad, hid, BLOCKS)
    grad, deriv_o = lax.optimization_barrier((grad, deriv_o))
    grad = lax.psum_scatter(
        grad, ("z", "c"), scatter_dimension=0, tiled=True, axis_index_groups=orders
    )

    back = sent_back(deriv, deriv_o, weights, weights_o, hid, BLOCKS)
    back = lax.all_to_all(
        back.reshape(n_chip, block, width), "p", split_axis=0, concat_axis=0, tiled=True
    ).reshape(n_chip * block, width)
    near, far = unpacked(unpick, gate2, back)
    far = lax.ppermute(far, "c", SWAP)
    scale = (tok_rows * n_data * n_chip * n_core * routes.shape[1] / EXPERTS) ** (-0.5)
    new = updated(
        grad, (w_gate_up, m_gate_up, v_gate_up), (w_down.T, m_down.T, v_down.T), scale, UPDATE_BLOCKS
    )
    new_wu, new_mu, new_vu = new[:3]
    new_wd, new_md, new_vd = (a.T for a in new[3:])
    far, new_mu = lax.optimization_barrier((far, new_mu))
    outputs, input_grads = joined(c, near, far)
    return (outputs, input_grads, new_wu, new_mu, new_vu, new_wd, new_md, new_vd)


def solution(mesh):
    n_data, n_expert = (mesh.shape[a] for a in ("dp", "expert"))
    cores = Mesh(mesh.devices.reshape(n_data, n_expert // 2, 2), ("z", "p", "c"))
    rows = P(("z", "p", "c"), None)
    up, down = P(None, "z", ("p", "c")), P(("p", "c"), "z")
    return jax.shard_map(
        shards,
        mesh=cores,
        in_specs=(rows, rows, rows, rows, up, down, up, up, down, down),
        out_specs=(rows, rows, up, up, up, down, down, down),
        check_vma=False,
    )
```

```python
import functools

import jax
import jax.numpy as jnp
from jax import lax
from jax.experimental import pallas as pl
from jax.experimental.pallas import tpu as pltpu
from jax.sharding import Mesh, PartitionSpec as P

EXPERTS = 8
CAPACITY = 20


first_decay = 0.9
second_decay = 0.95
first_correction = 1.0 - 0.9**50 * 0.9**50
second_correction = 1.0 - 0.95**50 * 0.95**50
learn_rate = 0.01
adam_epsilon = 1e-08

SWAP = [(0, 1), (1, 0)]
BLOCKS = 2


def slots_of(flat_routes):
    n = flat_routes.shape[0]
    onehot = (flat_routes[:, None] == jnp.arange(EXPERTS, dtype=jnp.int32)[None, :]).astype(jnp.bfloat16)
    earlier = (jnp.arange(n)[:, None] > jnp.arange(n)[None, :]).astype(jnp.bfloat16)
    before = jnp.dot(earlier, onehot, preferred_element_type=jnp.float32)
    return jnp.sum(before * onehot.astype(jnp.float32), axis=1).astype(jnp.int32)


def adam_update(weight, moment, second, grad_sum, scale):
    grad = grad_sum * scale
    moment_new = first_decay * moment + (1.0 - first_decay) * grad
    second_new = second_decay * second + (1.0 - second_decay) * grad * grad
    update = (
        moment_new / first_correction / (jnp.sqrt(second_new / second_correction) + adam_epsilon)
    )
    weight_new = (weight.astype(jnp.float32) - learn_rate * update).astype(jnp.bfloat16)
    return (weight_new, moment_new, second_new)


def dot(a, b, dims=((1,), (0,))):
    return lax.dot_general(a, b, (dims, ((), ())), preferred_element_type=jnp.float32)


MIB = 1 << 20
UPDATE_BLOCKS = 2
BACK_BLOCKS = 1
FIRST_VMEM = 56
VMEM = 56
BACK_VMEM = 28
LANES = 128


def in_hbm(array):
    return pltpu.with_memory_space_constraint(array, pltpu.HBM)


def in_vmem(array):
    return pltpu.with_memory_space_constraint(array, pltpu.VMEM)


def call(body, grid, in_specs, out_specs, out_shape, flops, scratch=(), vmem=VMEM, size=12 * MIB):
    return pl.pallas_call(
        body,
        grid=(grid,),
        in_specs=in_specs,
        out_specs=out_specs,
        out_shape=out_shape,
        scratch_shapes=list(scratch),
        compiler_params=pltpu.CompilerParams(vmem_limit_bytes=vmem * MIB),
        cost_estimate=pl.CostEstimate(flops=flops, bytes_accessed=size, transcendentals=0),
    )


def lay_body(up_ref, down_ref, out_ref):
    hid = down_ref.shape[1]
    out_ref[:, :hid] = up_ref[0]
    out_ref[:, hid : 2 * hid] = up_ref[1]
    out_ref[:, 2 * hid :] = down_ref[...]


def laid(up, down):
    rows, hid = down.shape
    return call(
        lay_body,
        1,
        [
            pl.BlockSpec((2, rows, hid), lambda i: (0, 0, 0)),
            pl.BlockSpec((rows, hid), lambda i: (0, 0)),
        ],
        pl.BlockSpec((rows, 3 * hid), lambda i: (0, 0)),
        jax.ShapeDtypeStruct((rows, 3 * hid), up.dtype),
        flops=up.size,
        vmem=56,
    )(up, down)


def pre_body(hid, x_ref, y_ref, w_ref, acc_ref):
    @pl.when(pl.program_id(0) == 0)
    def _():
        acc_ref[...] = jnp.zeros_like(acc_ref)

    acc_ref[:, : 2 * hid] += dot(x_ref[...], w_ref[:, : 2 * hid])
    acc_ref[:, 2 * hid :] += dot(y_ref[...], w_ref[:, 2 * hid :])


def first_half(rows, weights, hid, blocks):
    n, width = rows.shape
    cols = width // 2 // blocks
    return call(
        functools.partial(pre_body, hid),
        blocks,
        [
            pl.BlockSpec((n, cols), lambda i: (0, i)),
            pl.BlockSpec((n, cols), lambda i: (0, blocks + i)),
            pl.BlockSpec((cols, 3 * hid), lambda i: (i, 0)),
        ],
        pl.BlockSpec((n, 3 * hid), lambda i: (0, 0)),
        pltpu.VMEM((n, 3 * hid), jnp.float32),
        flops=n * hid,
        vmem=FIRST_VMEM,
        size=MIB >> 4,
    )(in_hbm(rows), in_hbm(rows), in_hbm(weights))


def write_grads(hid, x, y, deriv_ref, grad_ref):
    grad_ref[:, : 2 * hid] = dot(x, deriv_ref[:, : 2 * hid], ((0,), (0,))).astype(jnp.bfloat16)
    grad_ref[:, 2 * hid :] = dot(y, deriv_ref[:, 2 * hid :], ((0,), (0,))).astype(jnp.bfloat16)


def mid_body(hid, blocks, pre_ref, x_ref, y_ref, w_ref, deriv_ref, grad_ref, acc_ref):
    step = pl.program_id(0)

    @pl.when(step == 0)
    def _():
        acc_ref[...] = pre_ref[...]

    @pl.when(step < blocks)
    def _():
        acc_ref[:, : 2 * hid] += dot(x_ref[...], w_ref[:, : 2 * hid])
        acc_ref[:, 2 * hid :] += dot(y_ref[...], w_ref[:, 2 * hid :])

    @pl.when(step == blocks - 1)
    def _():
        act, linear, d_hidden = (acc_ref[:, k * hid : (k + 1) * hid] for k in range(3))
        sig = jax.nn.sigmoid(act)
        gated = act * sig
        deriv_ref[:, :hid] = (d_hidden * linear * sig * (1.0 + act * (1.0 - sig))).astype(jnp.bfloat16)
        deriv_ref[:, hid : 2 * hid] = (d_hidden * gated).astype(jnp.bfloat16)
        deriv_ref[:, 2 * hid :] = (gated * linear).astype(jnp.bfloat16)

    @pl.when(step >= blocks)
    def _():
        write_grads(hid, x_ref[...], y_ref[...], deriv_ref, grad_ref)


def second_half(pre, rows, weights, hid, blocks):
    n, width = rows.shape
    cols = width // 2 // blocks

    def at(i):
        return jnp.minimum(i, 2 * blocks - 1 - i)

    return call(
        functools.partial(mid_body, hid, blocks),
        2 * blocks,
        [
            pl.BlockSpec((n, 3 * hid), lambda i: (0, 0)),
            pl.BlockSpec((n, cols), lambda i: (0, at(i))),
            pl.BlockSpec((n, cols), lambda i: (0, blocks + at(i))),
            pl.BlockSpec((cols, 3 * hid), lambda i: (blocks + jnp.minimum(i, blocks - 1), 0)),
        ],
        [
            pl.BlockSpec((n, 3 * hid), lambda i: (0, 0)),
            pl.BlockSpec((cols, 3 * hid), lambda i: (blocks + jnp.minimum(blocks - 1, 2 * blocks - 1 - i), 0)),
        ],
        [
            pltpu.VMEM((n, 3 * hid), jnp.bfloat16),
            pltpu.HBM((width, 3 * hid), jnp.bfloat16),
        ],
        flops=6 * n * width * hid,
        scratch=[pltpu.VMEM((n, 3 * hid), jnp.float32)],
    )(in_vmem(pre), in_hbm(rows), in_hbm(rows), in_hbm(weights))


def grad_body(hid, x_ref, y_ref, deriv_ref, _, grad_ref):
    write_grads(hid, x_ref[...], y_ref[...], deriv_ref, grad_ref)


def first_grads(rows, deriv, grad, hid, blocks):
    n, width = rows.shape
    cols = width // 2 // blocks
    return pl.pallas_call(
        functools.partial(grad_body, hid),
        grid=(blocks,),
        in_specs=[
            pl.BlockSpec((n, cols), lambda i: (0, i)),
            pl.BlockSpec((n, cols), lambda i: (0, blocks + i)),
            pl.BlockSpec((n, 3 * hid), lambda i: (0, 0)),
            pl.BlockSpec(memory_space=pl.ANY),
        ],
        out_specs=pl.BlockSpec((cols, 3 * hid), lambda i: (i, 0)),
        out_shape=pltpu.HBM((width, 3 * hid), jnp.bfloat16),
        input_output_aliases={3: 0},
        compiler_params=pltpu.CompilerParams(vmem_limit_bytes=VMEM * MIB),
        cost_estimate=pl.CostEstimate(flops=3 * n * width * hid, bytes_accessed=12 * MIB, transcendentals=0),
    )(in_hbm(rows), in_hbm(rows), in_vmem(deriv), in_hbm(grad))


def back_body(hid, deriv_m_ref, deriv_o_ref, w_m_ref, w_o_ref, back_ref):
    def write(cols):
        mine = dot(deriv_m_ref[:, cols], w_m_ref[:, cols], ((1,), (1,)))
        other = dot(deriv_o_ref[:, cols], w_o_ref[:, cols], ((1,), (1,)))
        back_ref[...] = (mine + other).astype(jnp.bfloat16)

    @pl.when(lax.rem(pl.program_id(0), 2) == 0)
    def _():
        write(slice(2 * hid, 3 * hid))

    @pl.when(lax.rem(pl.program_id(0), 2) == 1)
    def _():
        write(slice(0, 2 * hid))


def sent_back(deriv_m, deriv_o, w_m, w_o, hid, blocks):
    n, width = deriv_m.shape[0], w_m.shape[0]
    cols = width // 2 // blocks
    deriv = pl.BlockSpec((n, 3 * hid), lambda i: (0, 0))
    return call(
        functools.partial(back_body, hid),
        2 * blocks,
        [
            deriv,
            deriv,
            pl.BlockSpec((cols, 3 * hid), lambda i: (lax.div(i, 2), 0)),
            pl.BlockSpec((cols, 3 * hid), lambda i: (blocks + lax.div(i, 2), 0)),
        ],
        pl.BlockSpec((n, cols), lambda i: (0, lax.div(i, 2) + blocks * lax.rem(i, 2))),
        pltpu.VMEM((n, width), jnp.bfloat16),
        flops=6 * n * width * hid,
        vmem=BACK_VMEM,
    )(in_vmem(deriv_m), in_vmem(deriv_o), in_hbm(w_m), in_hbm(w_o))


def unpack_body(pick_ref, gate_ref, back_ref, near_ref, far_ref):
    n = near_ref.shape[0]
    picked = dot(pick_ref[...], back_ref[...])
    picked = picked * jnp.where(pl.program_id(0) == 0, gate_ref[:, :1], 1.0)
    near_ref[...] = picked[:n].astype(jnp.bfloat16)
    far_ref[...] = picked[n:].astype(jnp.bfloat16)


def unpacked(pick, gate, back):
    tokens, rows = pick.shape
    half = back.shape[1] // 2
    result = pl.BlockSpec((tokens // 2, half), lambda i: (0, i))
    shape = jax.ShapeDtypeStruct((tokens // 2, 2 * half), jnp.bfloat16)
    return call(
        unpack_body,
        2,
        [
            pl.BlockSpec((tokens, rows), lambda i: (0, 0)),
            pl.BlockSpec((tokens, LANES), lambda i: (0, 0)),
            pl.BlockSpec((rows, half), lambda i: (0, i)),
        ],
        [result, result],
        [shape, shape],
        flops=4 * tokens * rows * half,
        vmem=20,
    )(pick, gate, back)


def update_body(scale, grad_ref, wu_ref, mu_ref, vu_ref, wd_ref, md_ref, vd_ref, *out_refs):
    hid = wd_ref.shape[1]
    for k, (w_ref, m_ref, v_ref) in enumerate(((wu_ref, mu_ref, vu_ref),) * 2 + ((wd_ref, md_ref, vd_ref),)):
        at = (k,) if k < 2 else ()
        grad = grad_ref[:, k * hid : (k + 1) * hid].astype(jnp.float32)
        new = adam_update(w_ref[at + (...,)], m_ref[at + (...,)], v_ref[at + (...,)], grad, scale)
        for ref, value in zip(out_refs[:3] if k < 2 else out_refs[3:], new):
            ref[at + (...,)] = value


def updated(grad, up, down, scale, blocks):
    rows, hid = down[0].shape
    step = rows // blocks
    up_spec = pl.BlockSpec((2, step, hid), lambda i: (0, i, 0))
    down_spec = pl.BlockSpec((step, hid), lambda i: (i, 0))
    return call(
        functools.partial(update_body, scale),
        blocks,
        [pl.BlockSpec((step, 3 * hid), lambda i: (i, 0))] + [up_spec] * 3 + [down_spec] * 3,
        [up_spec] * 3 + [down_spec] * 3,
        [jax.ShapeDtypeStruct(a.shape, a.dtype) for a in (*up, *down)],
        flops=60 * rows * hid,
        vmem=56,
    )(grad, *up, *down)


def join_body(core_ref, near_ref, far_ref, out_ref, grad_ref):
    half = near_ref.shape[1] // 2
    first = core_ref[0] == 0
    for ref, cols in ((out_ref, slice(0, half)), (grad_ref, slice(half, 2 * half))):
        near, far = near_ref[:, cols], far_ref[:, cols]
        ref[:, :half] = jnp.where(first, near, far)
        ref[:, half:] = jnp.where(first, far, near)


def joined(core, near, far):
    whole = pl.BlockSpec(near.shape, lambda i: (0, 0))
    shape = jax.ShapeDtypeStruct(near.shape, jnp.bfloat16)
    return call(
        join_body,
        1,
        [pl.BlockSpec(memory_space=pltpu.SMEM), whole, whole],
        [whole, whole],
        [shape, shape],
        flops=near.size,
        vmem=20,
    )(core.reshape(1), near, far)


def shards(
    tokens, cotangent, routes, gates, w_gate_up, w_down, m_gate_up, v_gate_up, m_down, v_down
):
    n_data, n_chip, n_core = (lax.axis_size(a) for a in ("z", "p", "c"))
    pair = n_chip // EXPERTS
    tok_rows, width = tokens.shape
    half = width // n_core
    block = n_core * CAPACITY
    hid = w_down.shape[0]
    c = lax.axis_index("c")
    orders = [
        [((z + k * n_data // n_core) % n_data) * n_core + k for z in range(n_data)]
        for k in range(n_core)
    ]

    owned = laid(w_gate_up, w_down.T)
    weights = lax.all_gather(owned, ("z", "c"), axis=0, tiled=True, axis_index_groups=orders)

    cot = (gates * cotangent.astype(jnp.float32)).astype(jnp.bfloat16)

    def half_of(array, k):
        return lax.dynamic_slice_in_dim(array, k * half, half, axis=1)

    def both_of(k):
        return jnp.concatenate([half_of(tokens, k), half_of(cot, k)], axis=1)

    sent, routes, gates = lax.optimization_barrier((both_of(1 - c), routes, gates))
    rows2 = jnp.concatenate([both_of(c), lax.ppermute(sent, "c", SWAP)], axis=0)
    flat = routes.reshape(-1)
    place = flat * block + c * CAPACITY + slots_of(flat)
    info = jnp.concatenate([place.astype(jnp.float32)[:, None], gates], axis=1)
    info2 = jnp.concatenate([info, lax.ppermute(info, "c", SWAP)], axis=0)
    place2 = info2[:, 0].astype(jnp.int32)
    gate2 = info2[:, 1:2]
    row_id = lax.broadcasted_iota(jnp.int32, (EXPERTS, pair, block), 0) * block + (
        lax.broadcasted_iota(jnp.int32, (EXPERTS, pair, block), 2)
    )
    row_id = row_id.reshape(-1)
    pick = (row_id[:, None] == place2[None, :]).astype(jnp.bfloat16)
    packed = dot(pick, rows2).astype(jnp.bfloat16).reshape(n_chip, block, width)
    got = lax.all_to_all(packed, "p", split_axis=0, concat_axis=0, tiled=True)
    got, place2, gate2 = lax.optimization_barrier((got, place2, gate2))
    mine = got.reshape(n_chip * block, width)
    unpick = (place2[:, None] == row_id[None, :]).astype(jnp.bfloat16)
    gate2 = jnp.broadcast_to(gate2, (gate2.shape[0], LANES))
    other = lax.ppermute(mine, "c", SWAP)

    ready, unpick, gate2 = lax.optimization_barrier((mine, unpick, gate2))
    pre = first_half(ready, weights, hid, BLOCKS)
    pre, other, sent = lax.optimization_barrier((pre, other, weights))
    weights_o = lax.ppermute(sent, "c", SWAP)
    deriv, grad = second_half(pre, other, weights, hid, BLOCKS)
    deriv, weights_o = lax.optimization_barrier((deriv, weights_o))
    deriv_o = lax.ppermute(deriv, "c", SWAP)
    grad = first_grads(mine, deriv, grad, hid, BLOCKS)
    grad, deriv_o = lax.optimization_barrier((grad, deriv_o))
    grad = lax.psum_scatter(
        grad, ("z", "c"), scatter_dimension=0, tiled=True, axis_index_groups=orders
    )

    back = sent_back(deriv, deriv_o, weights, weights_o, hid, BACK_BLOCKS)
    back = lax.all_to_all(
        back.reshape(n_chip, block, width), "p", split_axis=0, concat_axis=0, tiled=True
    ).reshape(n_chip * block, width)
    near, far = unpacked(unpick, gate2, back)
    far = lax.ppermute(far, "c", SWAP)
    scale = (tok_rows * n_data * n_chip * n_core * routes.shape[1] / EXPERTS) ** (-0.5)
    new = updated(
        grad, (w_gate_up, m_gate_up, v_gate_up), (w_down.T, m_down.T, v_down.T), scale, UPDATE_BLOCKS
    )
    new_wu, new_mu, new_vu = new[:3]
    new_wd, new_md, new_vd = (a.T for a in new[3:])
    far, new_mu = lax.optimization_barrier((far, new_mu))
    outputs, input_grads = joined(c, near, far)
    return (outputs, input_grads, new_wu, new_mu, new_vu, new_wd, new_md, new_vd)


def solution(mesh):
    n_data, n_expert = (mesh.shape[a] for a in ("dp", "expert"))
    cores = Mesh(mesh.devices.reshape(n_data, n_expert // 2, 2), ("z", "p", "c"))
    rows = P(("z", "p", "c"), None)
    up, down = P(None, "z", ("p", "c")), P(("p", "c"), "z")
    return jax.shard_map(
        shards,
        mesh=cores,
        in_specs=(rows, rows, rows, rows, up, down, up, up, down, down),
        out_specs=(rows, rows, up, up, up, down, down, down),
        check_vma=False,
    )
```

```python
import functools

import jax
import jax.numpy as jnp
from jax import lax
from jax.experimental import pallas as pl
from jax.experimental.pallas import tpu as pltpu
from jax.sharding import Mesh, PartitionSpec as P

EXPERTS = 8
CAPACITY = 20


first_decay = 0.9
second_decay = 0.95
first_correction = 1.0 - 0.9**50 * 0.9**50
second_correction = 1.0 - 0.95**50 * 0.95**50
learn_rate = 0.01
adam_epsilon = 1e-08

SWAP = [(0, 1), (1, 0)]
BLOCKS = 2


def slots_of(flat_routes):
    n = flat_routes.shape[0]
    onehot = (flat_routes[:, None] == jnp.arange(EXPERTS, dtype=jnp.int32)[None, :]).astype(jnp.bfloat16)
    earlier = (jnp.arange(n)[:, None] > jnp.arange(n)[None, :]).astype(jnp.bfloat16)
    before = jnp.dot(earlier, onehot, preferred_element_type=jnp.float32)
    return jnp.sum(before * onehot.astype(jnp.float32), axis=1).astype(jnp.int32)


def adam_update(weight, moment, second, grad_sum, scale):
    grad = grad_sum * scale
    moment_new = first_decay * moment + (1.0 - first_decay) * grad
    second_new = second_decay * second + (1.0 - second_decay) * grad * grad
    update = (
        moment_new / first_correction / (jnp.sqrt(second_new / second_correction) + adam_epsilon)
    )
    weight_new = (weight.astype(jnp.float32) - learn_rate * update).astype(jnp.bfloat16)
    return (weight_new, moment_new, second_new)


def dot(a, b, dims=((1,), (0,))):
    return lax.dot_general(a, b, (dims, ((), ())), preferred_element_type=jnp.float32)


MIB = 1 << 20
UPDATE_BLOCKS = 2
BACK_BLOCKS = 1
FIRST_VMEM = 56
VMEM = 56
BACK_VMEM = 28
LANES = 128


def in_hbm(array):
    return pltpu.with_memory_space_constraint(array, pltpu.HBM)


def in_vmem(array):
    return pltpu.with_memory_space_constraint(array, pltpu.VMEM)


def call(body, grid, in_specs, out_specs, out_shape, flops, scratch=(), vmem=VMEM, size=12 * MIB):
    return pl.pallas_call(
        body,
        grid=(grid,),
        in_specs=in_specs,
        out_specs=out_specs,
        out_shape=out_shape,
        scratch_shapes=list(scratch),
        compiler_params=pltpu.CompilerParams(vmem_limit_bytes=vmem * MIB),
        cost_estimate=pl.CostEstimate(flops=flops, bytes_accessed=size, transcendentals=0),
    )


def lay_body(up_ref, down_ref, out_ref):
    hid = down_ref.shape[1]
    out_ref[:, :hid] = up_ref[0]
    out_ref[:, hid : 2 * hid] = up_ref[1]
    out_ref[:, 2 * hid :] = down_ref[...]


def laid(up, down):
    rows, hid = down.shape
    return call(
        lay_body,
        1,
        [
            pl.BlockSpec((2, rows, hid), lambda i: (0, 0, 0)),
            pl.BlockSpec((rows, hid), lambda i: (0, 0)),
        ],
        pl.BlockSpec((rows, 3 * hid), lambda i: (0, 0)),
        jax.ShapeDtypeStruct((rows, 3 * hid), up.dtype),
        flops=up.size,
        vmem=56,
    )(up, down)


def pre_body(hid, x_ref, y_ref, w_ref, acc_ref):
    @pl.when(pl.program_id(0) == 0)
    def _():
        acc_ref[...] = jnp.zeros_like(acc_ref)

    acc_ref[:, : 2 * hid] += dot(x_ref[...], w_ref[:, : 2 * hid])
    acc_ref[:, 2 * hid :] += dot(y_ref[...], w_ref[:, 2 * hid :])


def first_half(rows, weights, hid, blocks):
    n, width = rows.shape
    cols = width // 2 // blocks
    return call(
        functools.partial(pre_body, hid),
        blocks,
        [
            pl.BlockSpec((n, cols), lambda i: (0, i)),
            pl.BlockSpec((n, cols), lambda i: (0, blocks + i)),
            pl.BlockSpec((cols, 3 * hid), lambda i: (i, 0)),
        ],
        pl.BlockSpec((n, 3 * hid), lambda i: (0, 0)),
        pltpu.VMEM((n, 3 * hid), jnp.float32),
        flops=n * hid,
        vmem=FIRST_VMEM,
        size=MIB >> 4,
    )(in_hbm(rows), in_hbm(rows), in_hbm(weights))


def write_grads(hid, x, y, deriv_ref, grad_ref):
    grad_ref[:, : 2 * hid] = dot(x, deriv_ref[:, : 2 * hid], ((0,), (0,))).astype(jnp.bfloat16)
    grad_ref[:, 2 * hid :] = dot(y, deriv_ref[:, 2 * hid :], ((0,), (0,))).astype(jnp.bfloat16)


def mid_body(hid, blocks, pre_ref, x_ref, y_ref, w_ref, deriv_ref, grad_ref, acc_ref):
    step = pl.program_id(0)

    @pl.when(step == 0)
    def _():
        acc_ref[...] = pre_ref[...]

    @pl.when(step < blocks)
    def _():
        acc_ref[:, : 2 * hid] += dot(x_ref[...], w_ref[:, : 2 * hid])
        acc_ref[:, 2 * hid :] += dot(y_ref[...], w_ref[:, 2 * hid :])

    @pl.when(step == blocks - 1)
    def _():
        act, linear, d_hidden = (acc_ref[:, k * hid : (k + 1) * hid] for k in range(3))
        sig = jax.nn.sigmoid(act)
        gated = act * sig
        deriv_ref[:, :hid] = (d_hidden * linear * sig * (1.0 + act * (1.0 - sig))).astype(jnp.bfloat16)
        deriv_ref[:, hid : 2 * hid] = (d_hidden * gated).astype(jnp.bfloat16)
        deriv_ref[:, 2 * hid :] = (gated * linear).astype(jnp.bfloat16)

    @pl.when(step >= blocks)
    def _():
        write_grads(hid, x_ref[...], y_ref[...], deriv_ref, grad_ref)


def second_half(pre, rows, weights, hid, blocks):
    n, width = rows.shape
    cols = width // 2 // blocks

    def at(i):
        return jnp.minimum(i, 2 * blocks - 1 - i)

    return call(
        functools.partial(mid_body, hid, blocks),
        2 * blocks,
        [
            pl.BlockSpec((n, 3 * hid), lambda i: (0, 0)),
            pl.BlockSpec((n, cols), lambda i: (0, at(i))),
            pl.BlockSpec((n, cols), lambda i: (0, blocks + at(i))),
            pl.BlockSpec((cols, 3 * hid), lambda i: (blocks + jnp.minimum(i, blocks - 1), 0)),
        ],
        [
            pl.BlockSpec((n, 3 * hid), lambda i: (0, 0)),
            pl.BlockSpec((cols, 3 * hid), lambda i: (blocks + jnp.minimum(blocks - 1, 2 * blocks - 1 - i), 0)),
        ],
        [
            pltpu.VMEM((n, 3 * hid), jnp.bfloat16),
            pltpu.HBM((width, 3 * hid), jnp.bfloat16),
        ],
        flops=6 * n * width * hid,
        scratch=[pltpu.VMEM((n, 3 * hid), jnp.float32)],
    )(in_vmem(pre), in_hbm(rows), in_hbm(rows), in_hbm(weights))


def grad_body(hid, x_ref, y_ref, deriv_ref, _, grad_ref):
    write_grads(hid, x_ref[...], y_ref[...], deriv_ref, grad_ref)


def first_grads(rows, deriv, grad, hid, blocks):
    n, width = rows.shape
    cols = width // 2 // blocks
    return pl.pallas_call(
        functools.partial(grad_body, hid),
        grid=(blocks,),
        in_specs=[
            pl.BlockSpec((n, cols), lambda i: (0, i)),
            pl.BlockSpec((n, cols), lambda i: (0, blocks + i)),
            pl.BlockSpec((n, 3 * hid), lambda i: (0, 0)),
            pl.BlockSpec(memory_space=pl.ANY),
        ],
        out_specs=pl.BlockSpec((cols, 3 * hid), lambda i: (i, 0)),
        out_shape=pltpu.HBM((width, 3 * hid), jnp.bfloat16),
        input_output_aliases={3: 0},
        compiler_params=pltpu.CompilerParams(vmem_limit_bytes=VMEM * MIB),
        cost_estimate=pl.CostEstimate(flops=3 * n * width * hid, bytes_accessed=12 * MIB, transcendentals=0),
    )(in_hbm(rows), in_hbm(rows), in_vmem(deriv), in_hbm(grad))


def back_body(hid, deriv_m_ref, deriv_o_ref, w_m_ref, w_o_ref, back_ref):
    def write(cols):
        mine = dot(deriv_m_ref[:, cols], w_m_ref[:, cols], ((1,), (1,)))
        other = dot(deriv_o_ref[:, cols], w_o_ref[:, cols], ((1,), (1,)))
        back_ref[...] = (mine + other).astype(jnp.bfloat16)

    @pl.when(lax.rem(pl.program_id(0), 2) == 0)
    def _():
        write(slice(2 * hid, 3 * hid))

    @pl.when(lax.rem(pl.program_id(0), 2) == 1)
    def _():
        write(slice(0, 2 * hid))


def sent_back(deriv_m, deriv_o, w_m, w_o, hid, blocks):
    n, width = deriv_m.shape[0], w_m.shape[0]
    cols = width // 2 // blocks
    deriv = pl.BlockSpec((n, 3 * hid), lambda i: (0, 0))
    return call(
        functools.partial(back_body, hid),
        2 * blocks,
        [
            deriv,
            deriv,
            pl.BlockSpec((cols, 3 * hid), lambda i: (lax.div(i, 2), 0)),
            pl.BlockSpec((cols, 3 * hid), lambda i: (blocks + lax.div(i, 2), 0)),
        ],
        pl.BlockSpec((n, cols), lambda i: (0, lax.div(i, 2) + blocks * lax.rem(i, 2))),
        pltpu.VMEM((n, width), jnp.bfloat16),
        flops=6 * n * width * hid,
        vmem=BACK_VMEM,
    )(in_vmem(deriv_m), in_vmem(deriv_o), in_hbm(w_m), in_hbm(w_o))


def unpack_body(pick_ref, gate_ref, back_ref, near_ref, far_ref):
    n = near_ref.shape[0]
    picked = dot(pick_ref[...], back_ref[...])
    picked = picked * jnp.where(pl.program_id(0) == 0, gate_ref[:, :1], 1.0)
    near_ref[...] = picked[:n].astype(jnp.bfloat16)
    far_ref[...] = picked[n:].astype(jnp.bfloat16)


def unpacked(pick, gate, back):
    tokens, rows = pick.shape
    half = back.shape[1] // 2
    result = pl.BlockSpec((tokens // 2, half), lambda i: (0, i))
    shape = jax.ShapeDtypeStruct((tokens // 2, 2 * half), jnp.bfloat16)
    return call(
        unpack_body,
        2,
        [
            pl.BlockSpec((tokens, rows), lambda i: (0, 0)),
            pl.BlockSpec((tokens, LANES), lambda i: (0, 0)),
            pl.BlockSpec((rows, half), lambda i: (0, i)),
        ],
        [result, result],
        [shape, shape],
        flops=4 * tokens * rows * half,
        vmem=20,
    )(pick, gate, back)


def update_body(scale, grad_ref, wu_ref, mu_ref, vu_ref, wd_ref, md_ref, vd_ref, *out_refs):
    hid = wd_ref.shape[1]
    for k, (w_ref, m_ref, v_ref) in enumerate(((wu_ref, mu_ref, vu_ref),) * 2 + ((wd_ref, md_ref, vd_ref),)):
        at = (k,) if k < 2 else ()
        grad = grad_ref[:, k * hid : (k + 1) * hid].astype(jnp.float32)
        new = adam_update(w_ref[at + (...,)], m_ref[at + (...,)], v_ref[at + (...,)], grad, scale)
        for ref, value in zip(out_refs[:3] if k < 2 else out_refs[3:], new):
            ref[at + (...,)] = value


def updated(grad, up, down, scale, blocks):
    rows, hid = down[0].shape
    step = rows // blocks
    up_spec = pl.BlockSpec((2, step, hid), lambda i: (0, i, 0))
    down_spec = pl.BlockSpec((step, hid), lambda i: (i, 0))
    return call(
        functools.partial(update_body, scale),
        blocks,
        [pl.BlockSpec((step, 3 * hid), lambda i: (i, 0))] + [up_spec] * 3 + [down_spec] * 3,
        [up_spec] * 3 + [down_spec] * 3,
        [jax.ShapeDtypeStruct(a.shape, a.dtype) for a in (*up, *down)],
        flops=60 * rows * hid,
        vmem=56,
    )(grad, *up, *down)


def join_body(core_ref, near_ref, far_ref, out_ref, grad_ref):
    half = near_ref.shape[1] // 2
    first = core_ref[0] == 0
    for ref, cols in ((out_ref, slice(0, half)), (grad_ref, slice(half, 2 * half))):
        near, far = near_ref[:, cols], far_ref[:, cols]
        ref[:, :half] = jnp.where(first, near, far)
        ref[:, half:] = jnp.where(first, far, near)


def joined(core, near, far):
    rows = pl.BlockSpec((near.shape[0] // 2, near.shape[1]), lambda i: (i, 0))
    shape = jax.ShapeDtypeStruct(near.shape, jnp.bfloat16)
    return call(
        join_body,
        2,
        [pl.BlockSpec(memory_space=pltpu.SMEM), rows, rows],
        [rows, rows],
        [shape, shape],
        flops=near.size,
        vmem=20,
    )(core.reshape(1), near, far)


def shards(
    tokens, cotangent, routes, gates, w_gate_up, w_down, m_gate_up, v_gate_up, m_down, v_down
):
    n_data, n_chip, n_core = (lax.axis_size(a) for a in ("z", "p", "c"))
    pair = n_chip // EXPERTS
    tok_rows, width = tokens.shape
    half = width // n_core
    block = n_core * CAPACITY
    hid = w_down.shape[0]
    c = lax.axis_index("c")
    orders = [
        [((z + k * n_data // n_core) % n_data) * n_core + k for z in range(n_data)]
        for k in range(n_core)
    ]

    owned = laid(w_gate_up, w_down.T)
    weights = lax.all_gather(owned, ("z", "c"), axis=0, tiled=True, axis_index_groups=orders)

    cot = (gates * cotangent.astype(jnp.float32)).astype(jnp.bfloat16)

    def half_of(array, k):
        return lax.dynamic_slice_in_dim(array, k * half, half, axis=1)

    def both_of(k):
        return jnp.concatenate([half_of(tokens, k), half_of(cot, k)], axis=1)

    sent, routes, gates = lax.optimization_barrier((both_of(1 - c), routes, gates))
    rows2 = jnp.concatenate([both_of(c), lax.ppermute(sent, "c", SWAP)], axis=0)
    flat = routes.reshape(-1)
    place = flat * block + c * CAPACITY + slots_of(flat)
    info = jnp.concatenate([place.astype(jnp.float32)[:, None], gates], axis=1)
    info2 = jnp.concatenate([info, lax.ppermute(info, "c", SWAP)], axis=0)
    place2 = info2[:, 0].astype(jnp.int32)
    gate2 = info2[:, 1:2]
    row_id = lax.broadcasted_iota(jnp.int32, (EXPERTS, pair, block), 0) * block + (
        lax.broadcasted_iota(jnp.int32, (EXPERTS, pair, block), 2)
    )
    row_id = row_id.reshape(-1)
    pick = (row_id[:, None] == place2[None, :]).astype(jnp.bfloat16)
    packed = dot(pick, rows2).astype(jnp.bfloat16).reshape(n_chip, block, width)
    got = lax.all_to_all(packed, "p", split_axis=0, concat_axis=0, tiled=True)
    got, place2, gate2 = lax.optimization_barrier((got, place2, gate2))
    mine = got.reshape(n_chip * block, width)
    unpick = (place2[:, None] == row_id[None, :]).astype(jnp.bfloat16)
    gate2 = jnp.broadcast_to(gate2, (gate2.shape[0], LANES))
    other = lax.ppermute(mine, "c", SWAP)

    ready, unpick, gate2 = lax.optimization_barrier((mine, unpick, gate2))
    pre = first_half(ready, weights, hid, BLOCKS)
    pre, other, sent = lax.optimization_barrier((pre, other, weights))
    weights_o = lax.ppermute(sent, "c", SWAP)
    deriv, grad = second_half(pre, other, weights, hid, BLOCKS)
    deriv, weights_o = lax.optimization_barrier((deriv, weights_o))
    deriv_o = lax.ppermute(deriv, "c", SWAP)
    grad = first_grads(mine, deriv, grad, hid, BLOCKS)
    grad, deriv_o = lax.optimization_barrier((grad, deriv_o))
    grad = lax.psum_scatter(
        grad, ("z", "c"), scatter_dimension=0, tiled=True, axis_index_groups=orders
    )

    back = sent_back(deriv, deriv_o, weights, weights_o, hid, BACK_BLOCKS)
    back = lax.all_to_all(
        back.reshape(n_chip, block, width), "p", split_axis=0, concat_axis=0, tiled=True
    ).reshape(n_chip * block, width)
    near, far = unpacked(unpick, gate2, back)
    far = lax.ppermute(far, "c", SWAP)
    scale = (tok_rows * n_data * n_chip * n_core * routes.shape[1] / EXPERTS) ** (-0.5)
    new = updated(
        grad, (w_gate_up, m_gate_up, v_gate_up), (w_down.T, m_down.T, v_down.T), scale, UPDATE_BLOCKS
    )
    new_wu, new_mu, new_vu = new[:3]
    new_wd, new_md, new_vd = (a.T for a in new[3:])
    far, new_mu = lax.optimization_barrier((far, new_mu))
    outputs, input_grads = joined(c, near, far)
    return (outputs, input_grads, new_wu, new_mu, new_vu, new_wd, new_md, new_vd)


def solution(mesh):
    n_data, n_expert = (mesh.shape[a] for a in ("dp", "expert"))
    cores = Mesh(mesh.devices.reshape(n_data, n_expert // 2, 2), ("z", "p", "c"))
    rows = P(("z", "p", "c"), None)
    up, down = P(None, "z", ("p", "c")), P(("p", "c"), "z")
    return jax.shard_map(
        shards,
        mesh=cores,
        in_specs=(rows, rows, rows, rows, up, down, up, up, down, down),
        out_specs=(rows, rows, up, up, up, down, down, down),
        check_vma=False,
    )
```
